512 devices in a mesh: replica: 8 (over z_lo, core), fsdp: 64 (over x, y, z_hi).
Axes of the slice: x: 4, y: 4, z: 16 (z_hi: 4, z_lo: 4; z = z_hi * 4 + z_lo), core: 2. Of those that a mesh axis runs over, the one named last changes fastest.
Arguments:
- activations: bfloat16 [8, 8192, 4096], P('replica', 'fsdp'), may hold values from -6 to 6
- cotangent: bfloat16 [8, 8192, 512], P('replica', 'fsdp'), may hold values from -6 to 6
- weights: bfloat16 [8, 4096, 512], P('replica', 'fsdp'), may hold values from -0.09375 to 0.09375
- stale_params: bfloat16 [8, 4, 4096, 512], P('replica', None, 'fsdp'), may hold values from -0.09375 to 0.09375
- global_params: float32 [4, 4096, 512], P(None, 'fsdp'), may hold values from -0.09375 to 0.09375
- momentum: float32 [4, 4096, 512], P(None, 'fsdp'), may hold values from -0.3125 to 0.3125
- plan: int32 [1], replicated, may hold values from 0 to 999
Outputs:
- values_out: bfloat16 [8, 8192, 512], P('replica', 'fsdp')
- input_grad: bfloat16 [8, 8192, 4096], P('replica', 'fsdp')
- new_weights: bfloat16 [8, 4096, 512], P('replica', 'fsdp')
- new_global: float32 [4, 4096, 512], P(None, 'fsdp')
- new_momentum: float32 [4, 4096, 512], P(None, 'fsdp')
The draws below stay inside these ranges and needn't reach their ends.
All inputs are finite; a program needn't handle non-finite values.
Results may differ from the reference program's by a relative error of at most 0.001.
Values may be sent and summed in bfloat16 or wider, within the bound.
A program may use at most 64 MiB of HBM per device.

```python
import jax
import jax.numpy as jnp
from jax import lax

D = 4096
F = 512
FRAGS = 4
TOKENS = 8192
REPLICAS = 8


def levels(own_key, shape, pieces, smallest, top_value):
    def one(dim, shards_of):
        steps = jax.random.uniform(jax.random.fold_in(jax.random.fold_in(own_key, 6), dim), (shards_of,), jnp.float32, smallest / len(pieces), top_value / len(pieces))
        return jnp.repeat(jnp.exp(steps), shape[dim] // shards_of).reshape((-1,) + (1,) * (len(shape) - dim - 1))

    gain = one(*pieces[0])
    for cut in pieces[1:]:
        gain = gain * one(*cut)
    return gain


def normal_values(own_key, shape, width, most, shards=(), kind=jnp.bfloat16):
    array = width * jax.random.normal(own_key, shape, jnp.float32)
    if shards:
        array = array * levels(own_key, shape, shards, -0.22, 0.18)
    return jnp.clip(array, -most, most).astype(kind)


def setup_inputs(seed: int = 0) -> dict:
    streams_of = jax.random.split(jax.random.key(seed), 8)
    activations = normal_values(streams_of[0], (REPLICAS, TOKENS, D), 1.0, 6.0, ((0, 8), (1, 64)))
    cotangent = normal_values(streams_of[1], (REPLICAS, TOKENS, F), 1.0, 6.0, ((0, 8), (1, 64)))
    weights = normal_values(streams_of[2], (REPLICAS, D, F), D ** -0.5, 0.09375, ((0, 8), (1, 64)))
    stale_params = normal_values(streams_of[3], (REPLICAS, FRAGS, D, F), D ** -0.5, 0.09375, ((0, 8), (2, 64)))
    global_params = normal_values(streams_of[4], (FRAGS, D, F), D ** -0.5, 0.09375, ((1, 64),), jnp.float32)
    momentum = normal_values(streams_of[5], (FRAGS, D, F), 0.02, 0.3125, ((1, 64),), jnp.float32)
    plan = jax.random.randint(streams_of[6], (1,), 0, 1000).astype(jnp.int32)
    return {"activations": activations, "cotangent": cotangent, "weights": weights, "stale_params": stale_params, "global_params": global_params, "momentum": momentum, "plan": plan}


def reference(activations, cotangent, weights, stale_params, global_params, momentum, plan):
    def one_replica(args):
        inputs, grads, weight = args
        out = jnp.dot(inputs, weight, preferred_element_type=jnp.float32).astype(jnp.bfloat16)
        back = jnp.dot(grads, weight.T, preferred_element_type=jnp.float32).astype(jnp.bfloat16)
        weight_grad = jnp.dot(inputs.T, grads, preferred_element_type=jnp.float32)
        inner = weight.astype(jnp.float32) - 0.0002 * weight_grad
        return out, back, inner

    values_out, input_grad, inner = lax.map(one_replica, (activations, cotangent, weights))
    frag = plan[0] % FRAGS
    picked = (jnp.arange(FRAGS, dtype=jnp.int32) == frag)
    global_old = jnp.sum(jnp.where(picked[:, None, None], global_params, 0.0), axis=0)
    moment_old = jnp.sum(jnp.where(picked[:, None, None], momentum, 0.0), axis=0)
    stale = jnp.sum(jnp.where(picked[None, :, None, None], stale_params.astype(jnp.float32), 0.0), axis=1)
    mean_delta = jnp.sum(global_old[None] - stale, axis=0) / REPLICAS
    moment_f = 0.9 * moment_old + mean_delta
    global_f = global_old - 0.7 * (mean_delta + 0.9 * moment_f)
    new_global = jnp.where(picked[:, None, None], global_f[None], global_params)
    new_momentum = jnp.where(picked[:, None, None], moment_f[None], momentum)
    mixed = 0.5 * inner + 0.5 * global_f[None]
    return values_out, input_grad, mixed.astype(jnp.bfloat16), new_global, new_momentum
```

```python
import functools

import jax
import jax.numpy as jnp
from jax import lax
from jax.experimental import pallas as pl
from jax.experimental.pallas import tpu as pltpu
from jax.sharding import PartitionSpec as P

MESH = pl.DeviceIdType.MESH
F32 = jnp.float32
BF16 = jnp.bfloat16
T = 128
F = 512
B = 64
RATE = 0.0002


def kernel(
    plan_ref, act_ref, cot_ref, w_ref, stale_ref, glob_ref, mom_ref,
    values_ref, igrad_ref, neww_ref, newg_ref, newm_ref,
    actg, cotg, wg, dwp, yrs, zsum, zrs, vp, vrs, ig, vout, wout,
    stl, sel, selp, chip, rsr, sg, gin, minn, gout, mout,
    s_cot, r_cot, s_act, r_act, s_wz, r_wz, s_wy, r_wy, s_y, r_y, s_z, r_z,
    s_ig, r_ig, s_v, r_v, s_st, r_st, l_in, l_act, l_out,
):
    rep = lax.axis_index("replica")
    fs = lax.axis_index("fsdp")
    zl, core = rep // 2, rep % 2
    x, y, z = fs // 16, (fs // 4) % 4, fs % 4
    zz = z % 2
    pair = z // 2

    def at_x(d):
        return (rep, ((x + d) % 4) * 16 + y * 4 + z)

    def at_y(d):
        return (rep, x * 16 + ((y + d) % 4) * 4 + z)

    z_of = (z + 1 - 2 * zz, 3 - z, (z + 2) % 4)

    def at_z(k):
        return (rep, x * 16 + y * 4 + z_of[k])

    def at_zl(d):
        return (((zl + d) % 4) * 2 + core, fs)

    other_core = (zl * 2 + 1 - core, fs)

    def rdma(src, dst, send, recv, to):
        return pltpu.make_async_remote_copy(
            src_ref=src, dst_ref=dst, send_sem=send, recv_sem=recv, device_id=to, device_id_type=MESH
        )

    def rows(i, n):
        return pl.ds(pl.multiple_of(i * n, n), n)

    def channels(xx, yy, half):
        zp = half * pair + (1 - half) * (1 - pair)
        return pl.ds(pl.multiple_of(xx * 1024 + yy * 256 + zp * 128, 128), 128)

    loads = [
        pltpu.make_async_copy(stale_ref, stl, l_in.at[0]),
        pltpu.make_async_copy(glob_ref, gin, l_in.at[1]),
        pltpu.make_async_copy(mom_ref, minn, l_in.at[2]),
        pltpu.make_async_copy(cot_ref, cotg.at[rows(x, T)], l_in.at[3]),
        pltpu.make_async_copy(w_ref, wg.at[1, pl.ds(pl.multiple_of(y * 128 + zz * 64, 64), B)], l_in.at[4]),
    ]
    for c in loads:
        c.start()
    for half in (0, 1):
        for yy in range(4):
            pltpu.make_async_copy(
                act_ref.at[:, channels(x, yy, half)], actg.at[half, rows(x, T), pl.ds(yy * 128, 128)], l_act.at[half]
            ).start()

    barrier = pltpu.get_barrier_semaphore()
    greet = [at_x(d) for d in (1, 2, 3)] + [at_y(d) for d in (1, 2, 3)] + [at_z(k) for k in range(3)]
    greet += [at_zl(d) for d in (1, 2, 3)] + [other_core]
    for to in greet:
        pl.semaphore_signal(barrier, inc=1, device_id=to, device_id_type=MESH)
    pl.semaphore_wait(barrier, len(greet))

    ORDER = (1, 3, 2)
    cots = [rdma(cot_ref, cotg.at[rows(x, T)], s_cot.at[d - 1], r_cot.at[d - 1], at_x(d)) for d in (1, 2, 3)]
    for d in ORDER:
        cots[d - 1].start()

    def w_rows(zpar):
        return pl.ds(pl.multiple_of(y * 128 + zpar * 64, 64), B)

    wz = [
        rdma(w_ref, wg.at[1 if k == 0 else 0, w_rows(zz)], s_wz.at[k], r_wz.at[k], at_z(k)) for k in range(3)
    ]
    for k in range(3):
        wz[k].start()
    slots = ((1, zz), (1, 1 - zz), (0, 1 - zz), (0, zz))

    def wy(slot, d):
        half, zpar = slots[slot]
        there = wg.at[half, w_rows(zpar)]
        return rdma(w_ref if slot == 0 else there, there, s_wy.at[slot, d - 1], r_wy.at[slot, d - 1], at_y(d))

    for d in ORDER:
        wy(0, d).start()

    def act_send(half, yy, d):
        return rdma(
            act_ref.at[:, channels((x + d) % 4, yy, half)],
            actg.at[half, rows(x, T), pl.ds(yy * 128, 128)],
            s_act.at[half, d - 1],
            r_act.at[half, d - 1],
            at_x(d),
        )

    for half in (0, 1):
        for yy in range(4):
            for d in ORDER:
                act_send(half, yy, d).start()

    def act_all(half, d):
        there = actg.at[half, rows(x, T)]
        return rdma(there, there, s_act.at[half, d - 1], r_act.at[half, d - 1], at_x(d))

    frag = plan_ref[0] % 4
    loads[0].wait()
    picked = jnp.zeros((B, F), F32)
    for k in range(4):
        picked = jnp.where(frag == k, stl[k].astype(F32), picked)
    sel[...] = picked.astype(BF16)
    to_core = rdma(sel, selp, s_st.at[0], r_st.at[0], other_core)
    to_core.start()
    to_core.wait_recv()
    chip[...] = (sel[...].astype(F32) + selp[...].astype(F32)).reshape(4, 2, 8, F)
    scatter = [
        rdma(chip.at[(zl + d) % 4, core], rsr.at[d - 1], s_st.at[d], r_st.at[d], at_zl(d)) for d in (1, 2, 3)
    ]
    for c in scatter:
        c.start()

    def pass_on(k):
        wz[k].wait_recv()
        for d in ORDER:
            wy(k + 1, d).start()

    pass_on(0)

    for c in scatter:
        c.wait_recv()
    sg[zl, core] = chip[zl, core] + rsr[0] + rsr[1] + rsr[2]
    spread = [
        rdma(sg.at[zl, core], sg.at[zl, core], s_st.at[3 + d], r_st.at[3 + d], at_zl(d)) for d in (1, 2, 3)
    ]
    for c in spread:
        c.start()

    pass_on(1)
    loads[3].wait()
    for c in cots:
        c.wait_recv()

    def y_send(half, zpar, d):
        to = (y + d) % 4
        return rdma(
            dwp.at[half, pl.ds(pl.multiple_of(to * 128 + zpar * 64, 64), B)],
            yrs.at[half, zpar, d - 1],
            s_y.at[half, zpar, d - 1],
            r_y.at[half, zpar, d - 1],
            at_y(d),
        )

    def weight_grad(half, first):
        whole = actg.at[half, rows(x, T)]
        pltpu.make_async_copy(whole, whole, l_act.at[half]).wait()
        for d in ORDER:
            act_all(half, d).wait_recv()

        def step(i, carry):
            yy = (y + 2 + i) % 4
            cols = pl.ds(pl.multiple_of(yy * 128, 128), 128)
            dwp[half, cols] = lax.dot_general(
                actg[half, :, cols], cotg[...], (((0,), (0,)), ((), ())), preferred_element_type=F32
            )
            return carry

        lax.fori_loop(0, 4, step, 0)
        for zpar in (first, 1 - first):
            for d in ORDER:
                y_send(half, zpar, d).start()

    weight_grad(0, zz)

    def ig_send(half, yy, d):
        return rdma(
            ig.at[half, rows((x + d) % 4, T), pl.ds(yy * 128, 128)],
            igrad_ref.at[:, channels(x, yy, half)],
            s_ig.at[half, d - 1],
            r_ig.at[half, d - 1],
            at_x(d),
        )

    def input_grad(half):
        def step(i, carry):
            block = rows((x + 2 + i) % 4, T)
            ig[half, block] = lax.dot_general(
                cotg[block], wg[half], (((1,), (1,)), ((), ())), preferred_element_type=F32
            ).astype(BF16)
            return carry

        lax.fori_loop(0, 4, step, 0)
        for yy in range(4):
            for d in ORDER:
                ig_send(half, yy, d).start()
            pltpu.make_async_copy(
                ig.at[half, rows(x, T), pl.ds(yy * 128, 128)], igrad_ref.at[:, channels(x, yy, half)], l_out.at[half]
            ).start()

    loads[4].wait()
    for slot in (0, 1):
        for d in ORDER:
            wy(slot, d).wait_recv()
    input_grad(1)

    pass_on(2)
    weight_grad(1, 1 - zz)

    def z_send(k):
        return rdma(zsum.at[k], zrs.at[k], s_z.at[k], r_z.at[k], at_z(k))

    def over_y(half, zpar):
        for d in ORDER:
            y_send(half, zpar, d).wait_recv()
        mine = dwp[half, pl.ds(pl.multiple_of(y * 128 + zpar * 64, 64), B)]
        return mine + yrs[half, zpar, 0] + yrs[half, zpar, 1] + yrs[half, zpar, 2]

    zsum[2] = over_y(0, zz)
    z_send(2).start()

    for slot in (2, 3):
        for d in ORDER:
            wy(slot, d).wait_recv()
    input_grad(0)

    def values_step(i, carry):
        block = rows((x + 1 + i) % 4, T)
        vp[block] = jnp.dot(actg[0, block], wg[0], preferred_element_type=F32) + jnp.dot(
            actg[1, block], wg[1], preferred_element_type=F32
        )
        return carry

    lax.fori_loop(0, 4, values_step, 0)

    def v_send(d):
        return rdma(vp.at[rows((x + d) % 4, T)], vrs.at[d - 1], s_v.at[d - 1], r_v.at[d - 1], at_x(d))

    for d in ORDER:
        v_send(d).start()

    zsum[1] = over_y(0, 1 - zz)
    z_send(1).start()
    zsum[0] = over_y(1, 1 - zz)
    z_send(0).start()

    for c in spread:
        c.wait_recv()
    across = rdma(sg.at[:, core], sg.at[:, core], s_st.at[7], r_st.at[7], other_core)
    across.start()
    across.wait_recv()
    loads[1].wait()
    loads[2].wait()
    old = jnp.zeros((B, F), F32)
    moment = jnp.zeros((B, F), F32)
    for k in range(4):
        old = jnp.where(frag == k, gin[k], old)
        moment = jnp.where(frag == k, minn[k], moment)
    mean = old - sg[...].reshape(B, F) / 8.0
    moment = 0.9 * moment + mean
    new = old - 0.7 * (mean + 0.9 * moment)
    for k in range(4):
        gout[k] = jnp.where(frag == k, new, gin[k])
        mout[k] = jnp.where(frag == k, moment, minn[k])
    stores = [
        pltpu.make_async_copy(gout, newg_ref, l_out.at[2]),
        pltpu.make_async_copy(mout, newm_ref, l_out.at[3]),
    ]
    stores[0].start()
    stores[1].start()

    zsum[3] = over_y(1, zz)

    for d in ORDER:
        v_send(d).wait_recv()
    vout[...] = (vp[rows(x, T)] + vrs[0] + vrs[1] + vrs[2]).astype(BF16)
    stores.append(pltpu.make_async_copy(vout, values_ref, l_out.at[4]))
    stores[2].start()

    for k in range(3):
        z_send(k).wait_recv()
    grad = zsum[3] + zrs[0] + zrs[1] + zrs[2]
    inner = wg[1, w_rows(zz)].astype(F32) - RATE * grad
    picked = jnp.zeros((B, F), F32)
    for k in range(4):
        picked = jnp.where(frag == k, gout[k], picked)
    wout[...] = (0.5 * inner + 0.5 * picked).astype(BF16)
    stores.append(pltpu.make_async_copy(wout, neww_ref, l_out.at[5]))
    stores[3].start()

    for half in (0, 1):
        landed = igrad_ref.at[:, pl.ds(0, 512)]
        for d in (1, 2, 3):
            own = ig.at[half, rows((x + d) % 4, T)]
            back = rdma(own, landed, s_ig.at[half, d - 1], r_ig.at[half, d - 1], at_x(d))
            back.wait_recv()
            back.wait_send()
            act_all(half, d).wait_send()
        pltpu.make_async_copy(ig.at[half, rows(x, T)], landed, l_out.at[half]).wait()
    for c in cots + wz + scatter + spread + [to_core, across]:
        c.wait_send()
    for d in (1, 2, 3):
        v_send(d).wait_send()
        for slot in range(4):
            wy(slot, d).wait_send()
        for half in (0, 1):
            for zpar in (0, 1):
                y_send(half, zpar, d).wait_send()
    for k in range(3):
        z_send(k).wait_send()
    for c in stores:
        c.wait()


def per_device(activations, cotangent, weights, stale_params, global_params, momentum, plan):
    anywhere = pl.BlockSpec(memory_space=pl.ANY)
    dma = pltpu.SemaphoreType.DMA
    outs = pl.pallas_call(
        kernel,
        name="diloco_step",
        out_shape=(
            jax.ShapeDtypeStruct((T, F), BF16),
            jax.ShapeDtypeStruct((T, 4096), BF16),
            jax.ShapeDtypeStruct((B, F), BF16),
            jax.ShapeDtypeStruct((4, B, F), F32),
            jax.ShapeDtypeStruct((4, B, F), F32),
        ),
        in_specs=[pl.BlockSpec(memory_space=pltpu.SMEM)] + [anywhere] * 6,
        out_specs=(anywhere,) * 5,
        scratch_shapes=[
            pltpu.VMEM((2, 512, 512), BF16),
            pltpu.VMEM((512, F), BF16),
            pltpu.VMEM((2, 512, F), BF16),
            pltpu.VMEM((2, 512, F), F32),
            pltpu.VMEM((2, 2, 3, B, F), F32),
            pltpu.VMEM((4, B, F), F32),
            pltpu.VMEM((3, B, F), F32),
            pltpu.VMEM((512, F), F32),
            pltpu.VMEM((3, T, F), F32),
            pltpu.VMEM((2, 512, 512), BF16),
            pltpu.VMEM((T, F), BF16),
            pltpu.VMEM((B, F), BF16),
            pltpu.VMEM((4, B, F), BF16),
            pltpu.VMEM((B, F), BF16),
            pltpu.VMEM((B, F), BF16),
            pltpu.VMEM((4, 2, 8, F), F32),
            pltpu.VMEM((3, 8, F), F32),
            pltpu.VMEM((4, 2, 8, F), F32),
            pltpu.VMEM((4, B, F), F32),
            pltpu.VMEM((4, B, F), F32),
            pltpu.VMEM((4, B, F), F32),
            pltpu.VMEM((4, B, F), F32),
            dma((3,)), dma((3,)),
            dma((2, 3)), dma((2, 3)),
            dma((3,)), dma((3,)),
            dma((4, 3)), dma((4, 3)),
            dma((2, 2, 3)), dma((2, 2, 3)),
            dma((3,)), dma((3,)),
            dma((2, 3)), dma((2, 3)),
            dma((3,)), dma((3,)),
            dma((8,)), dma((8,)),
            dma((5,)), dma((2,)), dma((6,)),
        ],
        compiler_params=pltpu.CompilerParams(
            collective_id=0, has_side_effects=True, vmem_limit_bytes=40 << 20
        ),
        cost_estimate=pl.CostEstimate(flops=1_700_000_000, bytes_accessed=7 << 20, transcendentals=0),
    )(plan, activations[0], cotangent[0], weights[0], stale_params[0], global_params, momentum)
    values, igrad, neww, newg, newm = outs
    return (values[None], igrad[None], neww[None], newg, newm)


def solution(mesh):
    placed = (
        P("replica", "fsdp", None),
        P("replica", "fsdp", None),
        P("replica", "fsdp", None),
        P("replica", None, "fsdp", None),
        P(None, "fsdp", None),
        P(None, "fsdp", None),
        P(),
    )
    return jax.shard_map(
        per_device,
        mesh=mesh,
        in_specs=placed,
        out_specs=(
            P("replica", "fsdp", None),
            P("replica", "fsdp", None),
            P("replica", "fsdp", None),
            P(None, "fsdp", None),
            P(None, "fsdp", None),
        ),
        check_vma=False,
    )
```

```python
import functools

import jax
import jax.numpy as jnp
from jax import lax
from jax.experimental import pallas as pl
from jax.experimental.pallas import tpu as pltpu
from jax.sharding import PartitionSpec as P

MESH = pl.DeviceIdType.MESH
F32 = jnp.float32
BF16 = jnp.bfloat16
T = 128
F = 512
B = 64
RATE = 0.0002


def kernel(
    plan_ref, act_ref, cot_ref, w_ref, stale_ref, glob_ref, mom_ref,
    values_ref, igrad_ref, neww_ref, newg_ref, newm_ref,
    actg, cotg, wg, dwp, brs, zsum, zrs, zfar, vp, vrs, ig, vout, wout,
    stl, sel, selp, chip, rsr, sg, gin, minn, gout, mout,
    s_cot, r_cot, s_act, r_act, s_wz, r_wz, s_wb, r_wb, s_b, r_b, s_z, r_z, s_zf, r_zf,
    s_ig, r_ig, s_v, r_v, s_st, r_st, l_in, l_act, l_out,
):
    rep = lax.axis_index("replica")
    fs = lax.axis_index("fsdp")
    zl, core = rep // 2, rep % 2
    x, y, z = fs // 16, (fs // 4) % 4, fs % 4
    step_a, step_b = 16 - 12 * core, 4 + 12 * core
    a, b = x + core * (y - x), y + core * (x - y)
    wide_a, wide_b = 1024 - 768 * core, 256 + 768 * core
    zz = z % 2
    pair = z // 2

    def at_a(d):
        return (rep, ((a + d) % 4) * step_a + b * step_b + z)

    def at_b(d):
        return (rep, a * step_a + ((b + d) % 4) * step_b + z)

    z_of = (z + 1 - 2 * zz, 3 - z)

    def at_z(k):
        return (rep, x * 16 + y * 4 + z_of[k])

    def at_zl(d):
        return (((zl + d) % 4) * 2 + core, fs)

    ORDER = (1, 3, 2)
    CHUNKS = (2, 1, 3, 0)
    other_core = (zl * 2 + 1 - core, fs)

    def rdma(src, dst, send, recv, to):
        return pltpu.make_async_remote_copy(
            src_ref=src, dst_ref=dst, send_sem=send, recv_sem=recv, device_id=to, device_id_type=MESH
        )

    def rows(i, n):
        return pl.ds(pl.multiple_of(i * n, n), n)

    def channels(aa, bb, half):
        zp = half * pair + (1 - half) * (1 - pair)
        return pl.ds(pl.multiple_of(aa * wide_a + bb * wide_b + zp * 128, 128), 128)

    def lanes(bb):
        return pl.ds(pl.multiple_of(bb * 128, 128), 128)

    loads = [
        pltpu.make_async_copy(stale_ref, stl, l_in.at[0]),
        pltpu.make_async_copy(glob_ref, gin, l_in.at[1]),
        pltpu.make_async_copy(mom_ref, minn, l_in.at[2]),
        pltpu.make_async_copy(cot_ref, cotg.at[rows(a, T)], l_in.at[3]),
        pltpu.make_async_copy(w_ref, wg.at[1, pl.ds(pl.multiple_of(b * 128 + zz * 64, 64), B)], l_in.at[4]),
    ]
    for c in loads:
        c.start()
    def act_own(half, j):
        bb = (b + CHUNKS[j]) % 4
        return pltpu.make_async_copy(
            act_ref.at[:, channels(a, bb, half)], actg.at[half, rows(a, T), lanes(bb)], l_act.at[half, j]
        )

    for half in (0, 1):
        for j in range(4):
            act_own(half, j).start()

    barrier = pltpu.get_barrier_semaphore()
    greet = [at_a(d) for d in (1, 2, 3)] + [at_b(d) for d in (1, 2, 3)] + [at_z(k) for k in range(2)]
    greet += [at_zl(d) for d in (1, 2, 3)] + [other_core]
    for to in greet:
        pl.semaphore_signal(barrier, inc=1, device_id=to, device_id_type=MESH)
    pl.semaphore_wait(barrier, len(greet))

    cots = [rdma(cot_ref, cotg.at[rows(a, T)], s_cot.at[d - 1], r_cot.at[d - 1], at_a(d)) for d in (1, 2, 3)]
    for d in ORDER:
        cots[d - 1].start()

    def w_rows(zpar):
        return pl.ds(pl.multiple_of(b * 128 + zpar * 64, 64), B)

    wz = [
        rdma(w_ref, wg.at[1 if k == 0 else 0, w_rows(zz)], s_wz.at[k], r_wz.at[k], at_z(k)) for k in range(2)
    ]
    for k in range(2):
        wz[k].start()
    slots = ((1, zz), (1, 1 - zz), (0, 1 - zz), (0, zz))

    def wb(slot, d):
        half, zpar = slots[slot]
        there = wg.at[half, w_rows(zpar)]
        return rdma(w_ref if slot == 0 else there, there, s_wb.at[slot, d - 1], r_wb.at[slot, d - 1], at_b(d))

    for d in ORDER:
        wb(0, d).start()

    def act_send(half, j, d):
        bb = (b + CHUNKS[j]) % 4
        return rdma(
            act_ref.at[:, channels((a + d) % 4, bb, half)],
            actg.at[half, rows(a, T), lanes(bb)],
            s_act.at[half, j, d - 1],
            r_act.at[half, j, d - 1],
            at_a(d),
        )

    for half in (0, 1):
        for j in range(4):
            for d in ORDER:
                act_send(half, j, d).start()

    frag = plan_ref[0] % 4
    loads[0].wait()
    picked = jnp.zeros((B, F), F32)
    for k in range(4):
        picked = jnp.where(frag == k, stl[k].astype(F32), picked)
    sel[...] = picked.astype(BF16)
    to_core = rdma(sel, selp, s_st.at[0], r_st.at[0], other_core)
    to_core.start()
    to_core.wait_recv()
    chip[...] = (sel[...].astype(F32) + selp[...].astype(F32)).reshape(4, 2, 8, F)
    scatter = [
        rdma(chip.at[(zl + d) % 4, core], rsr.at[d - 1], s_st.at[d], r_st.at[d], at_zl(d)) for d in (1, 2, 3)
    ]
    for c in scatter:
        c.start()

    def b_send(half, zpar, j):
        to = (b + CHUNKS[j]) % 4
        return rdma(
            dwp.at[half, pl.ds(pl.multiple_of(to * 128 + zpar * 64, 64), B)],
            brs.at[half, zpar, j],
            s_b.at[half, zpar, j],
            r_b.at[half, zpar, j],
            at_b(CHUNKS[j]),
        )

    def weight_grad(half, first):
        for j in range(4):
            act_own(half, j).wait()
            for d in ORDER:
                act_send(half, j, d).wait_recv()
            cols = lanes((b + CHUNKS[j]) % 4)
            dwp[half, cols] = lax.dot_general(
                actg[half, :, cols], cotg[...], (((0,), (0,)), ((), ())), preferred_element_type=F32
            )
            if j < 3:
                b_send(half, first, j).start()
                b_send(half, 1 - first, j).start()

    loads[3].wait()
    for c in cots:
        c.wait_recv()
    weight_grad(0, zz)

    def part(i, zpar, h):
        return wg.at[i, pl.ds(pl.multiple_of(b * 128 + zpar * 64 + h * 32, 32), B // 2)]

    wz2 = [
        rdma(part(1 - h, 1 - zz, h), part(0, 1 - zz, h), s_wz.at[2 + h], r_wz.at[2 + h], at_z(1 - h)) for h in (0, 1)
    ]

    def pass_on(slot):
        for d in ORDER:
            wb(slot, d).start()

    for k in (0, 1):
        wz[k].wait_recv()
        wz2[k].start()
        pass_on(k + 1)

    for c in scatter:
        c.wait_recv()
    sg[zl, core] = chip[zl, core] + rsr[0] + rsr[1] + rsr[2]
    spread = [
        rdma(sg.at[zl, core], sg.at[zl, core], s_st.at[3 + d], r_st.at[3 + d], at_zl(d)) for d in (1, 2, 3)
    ]
    for c in spread:
        c.start()

    weight_grad(1, 1 - zz)
    for c in wz2:
        c.wait_recv()
    pass_on(3)

    def halves(h):
        return pl.ds(h * 32, B // 2)

    def z_far(h):
        return rdma(zsum.at[2, halves(h)], zfar.at[h], s_zf.at[h], r_zf.at[h], at_z(1 - h))

    def z_send(k, h):
        return rdma(zsum.at[k, halves(h)], zrs.at[k, halves(h)], s_z.at[k, h], r_z.at[k, h], at_z(k))

    def over_b(half, zpar):
        for j in range(3):
            b_send(half, zpar, j).wait_recv()
        mine = dwp[half, pl.ds(pl.multiple_of(b * 128 + zpar * 64, 64), B)]
        return mine + brs[half, zpar, 0] + brs[half, zpar, 1] + brs[half, zpar, 2]

    def z_add(h):
        z_far(h).wait_recv()
        zsum[h, halves(h)] = zsum[h, halves(h)] + zfar[h]
        z_send(h, h).start()

    zsum[2] = over_b(0, zz)
    z_far(0).start()
    z_far(1).start()

    def ig_send(half, yy, d):
        return rdma(
            ig.at[half, rows((a + d) % 4, T), pl.ds(yy * 128, 128)],
            igrad_ref.at[:, channels(a, yy, half)],
            s_ig.at[half, d - 1],
            r_ig.at[half, d - 1],
            at_a(d),
        )

    def input_grad(half):
        ig[half] = lax.dot_general(
            cotg[...], wg[half], (((1,), (1,)), ((), ())), preferred_element_type=F32
        ).astype(BF16)
        for yy in range(4):
            for d in ORDER:
                ig_send(half, yy, d).start()
            pltpu.make_async_copy(
                ig.at[half, rows(a, T), pl.ds(yy * 128, 128)], igrad_ref.at[:, channels(a, yy, half)], l_out.at[half]
            ).start()

    loads[4].wait()
    for slot in (0, 1):
        for d in ORDER:
            wb(slot, d).wait_recv()
    input_grad(1)

    zsum[1] = over_b(0, 1 - zz)
    z_send(1, 0).start()
    zsum[0] = over_b(1, 1 - zz)
    z_send(0, 1).start()

    for slot in (2, 3):
        for d in ORDER:
            wb(slot, d).wait_recv()
    input_grad(0)

    vp[...] = jnp.dot(actg[0], wg[0], preferred_element_type=F32) + jnp.dot(
        actg[1], wg[1], preferred_element_type=F32
    )

    def v_send(d):
        return rdma(vp.at[rows((a + d) % 4, T)], vrs.at[d - 1], s_v.at[d - 1], r_v.at[d - 1], at_a(d))

    for d in ORDER:
        v_send(d).start()

    z_add(1)
    z_add(0)

    for c in spread:
        c.wait_recv()
    across = rdma(sg.at[:, core], sg.at[:, core], s_st.at[7], r_st.at[7], other_core)
    across.start()
    across.wait_recv()
    loads[1].wait()
    loads[2].wait()
    old = jnp.zeros((B, F), F32)
    moment = jnp.zeros((B, F), F32)
    for k in range(4):
        old = jnp.where(frag == k, gin[k], old)
        moment = jnp.where(frag == k, minn[k], moment)
    mean = old - sg[...].reshape(B, F) / 8.0
    moment = 0.9 * moment + mean
    new = old - 0.7 * (mean + 0.9 * moment)
    for k in range(4):
        gout[k] = jnp.where(frag == k, new, gin[k])
        mout[k] = jnp.where(frag == k, moment, minn[k])
    stores = [
        pltpu.make_async_copy(gout, newg_ref, l_out.at[2]),
        pltpu.make_async_copy(mout, newm_ref, l_out.at[3]),
    ]
    stores[0].start()
    stores[1].start()

    zsum[3] = over_b(1, zz)

    for d in ORDER:
        v_send(d).wait_recv()
    vout[...] = (vp[rows(a, T)] + vrs[0] + vrs[1] + vrs[2]).astype(BF16)
    stores.append(pltpu.make_async_copy(vout, values_ref, l_out.at[4]))
    stores[2].start()

    for k in (0, 1):
        for h in (0, 1):
            z_send(k, h).wait_recv()
    grad = zsum[3] + zrs[0] + zrs[1]
    inner = wg[1, w_rows(zz)].astype(F32) - RATE * grad
    picked = jnp.zeros((B, F), F32)
    for k in range(4):
        picked = jnp.where(frag == k, gout[k], picked)
    wout[...] = (0.5 * inner + 0.5 * picked).astype(BF16)
    stores.append(pltpu.make_async_copy(wout, neww_ref, l_out.at[5]))
    stores[3].start()

    for half in (0, 1):
        landed = igrad_ref.at[:, pl.ds(0, 512)]
        for d in (1, 2, 3):
            own = ig.at[half, rows((a + d) % 4, T)]
            back = rdma(own, landed, s_ig.at[half, d - 1], r_ig.at[half, d - 1], at_a(d))
            back.wait_recv()
            back.wait_send()
            for j in range(4):
                act_send(half, j, d).wait_send()
        pltpu.make_async_copy(ig.at[half, rows(a, T)], landed, l_out.at[half]).wait()
    for c in cots + wz + wz2 + scatter + spread + [to_core, across]:
        c.wait_send()
    for d in (1, 2, 3):
        v_send(d).wait_send()
        for slot in range(4):
            wb(slot, d).wait_send()
        for half in (0, 1):
            for zpar in (0, 1):
                b_send(half, zpar, d - 1).wait_send()
    for k in (0, 1):
        z_far(k).wait_send()
        for h in (0, 1):
            z_send(k, h).wait_send()
    for c in stores:
        c.wait()


def hand_out(*refs):
    ins, outs, vmem, arrived, left = refs[:5], refs[5:10], refs[10:15], refs[15], refs[16]
    come = [pltpu.make_async_copy(ins[i], vmem[i], arrived.at[i]) for i in range(5)]
    go = [pltpu.make_async_copy(vmem[i], outs[i], left.at[i]) for i in range(5)]
    for i in (1, 3, 4, 0, 2):
        come[i].start()
    for i in (1, 3, 4, 0, 2):
        come[i].wait()
        go[i].start()
    for i in range(5):
        go[i].wait()


def per_device(activations, cotangent, weights, stale_params, global_params, momentum, plan):
    anywhere = pl.BlockSpec(memory_space=pl.ANY)
    dma = pltpu.SemaphoreType.DMA
    outs = pl.pallas_call(
        kernel,
        name="diloco_step",
        out_shape=(
            jax.ShapeDtypeStruct((T, F), BF16),
            jax.ShapeDtypeStruct((T, 4096), BF16),
            jax.ShapeDtypeStruct((B, F), BF16),
            jax.ShapeDtypeStruct((4, B, F), F32),
            jax.ShapeDtypeStruct((4, B, F), F32),
        ),
        in_specs=[pl.BlockSpec(memory_space=pltpu.SMEM)] + [anywhere] * 6,
        out_specs=(anywhere,) * 5,
        scratch_shapes=[
            pltpu.VMEM((2, 512, 512), BF16),
            pltpu.VMEM((512, F), BF16),
            pltpu.VMEM((2, 512, F), BF16),
            pltpu.VMEM((2, 512, F), F32),
            pltpu.VMEM((2, 2, 3, B, F), F32),
            pltpu.VMEM((4, B, F), F32),
            pltpu.VMEM((2, B, F), F32),
            pltpu.VMEM((2, B // 2, F), F32),
            pltpu.VMEM((512, F), F32),
            pltpu.VMEM((3, T, F), F32),
            pltpu.VMEM((2, 512, 512), BF16),
            pltpu.VMEM((T, F), BF16),
            pltpu.VMEM((B, F), BF16),
            pltpu.VMEM((4, B, F), BF16),
            pltpu.VMEM((B, F), BF16),
            pltpu.VMEM((B, F), BF16),
            pltpu.VMEM((4, 2, 8, F), F32),
            pltpu.VMEM((3, 8, F), F32),
            pltpu.VMEM((4, 2, 8, F), F32),
            pltpu.VMEM((4, B, F), F32),
            pltpu.VMEM((4, B, F), F32),
            pltpu.VMEM((4, B, F), F32),
            pltpu.VMEM((4, B, F), F32),
            dma((3,)), dma((3,)),
            dma((2, 4, 3)), dma((2, 4, 3)),
            dma((4,)), dma((4,)),
            dma((4, 3)), dma((4, 3)),
            dma((2, 2, 3)), dma((2, 2, 3)),
            dma((2, 2)), dma((2, 2)),
            dma((2,)), dma((2,)),
            dma((2, 3)), dma((2, 3)),
            dma((3,)), dma((3,)),
            dma((8,)), dma((8,)),
            dma((5,)), dma((2, 4)), dma((6,)),
        ],
        compiler_params=pltpu.CompilerParams(
            collective_id=0, has_side_effects=True, vmem_limit_bytes=60 << 20
        ),
        cost_estimate=pl.CostEstimate(flops=1_700_000_000, bytes_accessed=7 << 20, transcendentals=0),
    )(plan, activations[0], cotangent[0], weights[0], stale_params[0], global_params, momentum)
    values, igrad, neww, newg, newm = pl.pallas_call(
        hand_out,
        name="hand_out",
        out_shape=tuple(jax.ShapeDtypeStruct(o.shape, o.dtype) for o in outs),
        in_specs=[anywhere] * 5,
        out_specs=(anywhere,) * 5,
        scratch_shapes=[pltpu.VMEM(o.shape, o.dtype) for o in outs] + [dma((5,)), dma((5,))],
        compiler_params=pltpu.CompilerParams(vmem_limit_bytes=60 << 20),
    )(*outs)
    return (values[None], igrad[None], neww[None], newg, newm)


def solution(mesh):
    placed = (
        P("replica", "fsdp", None),
        P("replica", "fsdp", None),
        P("replica", "fsdp", None),
        P("replica", None, "fsdp", None),
        P(None, "fsdp", None),
        P(None, "fsdp", None),
        P(),
    )
    return jax.shard_map(
        per_device,
        mesh=mesh,
        in_specs=placed,
        out_specs=(
            P("replica", "fsdp", None),
            P("replica", "fsdp", None),
            P("replica", "fsdp", None),
            P(None, "fsdp", None),
            P(None, "fsdp", None),
        ),
        check_vma=False,
    )
```

```python
import functools

import jax
import jax.numpy as jnp
from jax import lax
from jax.experimental import pallas as pl
from jax.experimental.pallas import tpu as pltpu
from jax.sharding import PartitionSpec as P

MESH = pl.DeviceIdType.MESH
F32 = jnp.float32
BF16 = jnp.bfloat16
T = 128
F = 512
B = 64
RATE = 0.0002


def kernel(
    plan_ref, act_ref, cot_ref, w_ref, stale_ref, glob_ref, mom_ref,
    values_ref, igrad_ref, neww_ref, newg_ref, newm_ref,
    actg, cotg, wg, dwp, brs, bfar, zsum, zrs, zfar, vp, vrs, ig, vout, wout,
    stl, sel, selp, chip, rsr, sg, gin, minn, gout, mout,
    s_cot, r_cot, s_act, r_act, s_wz, r_wz, s_wb, r_wb, s_wbf, r_wbf, s_b, r_b, s_bf, r_bf, s_z, r_z, s_zf, r_zf,
    s_ig, r_ig, s_v, r_v, s_st, r_st, l_in, l_act, l_out,
):
    rep = lax.axis_index("replica")
    fs = lax.axis_index("fsdp")
    zl, core = rep // 2, rep % 2
    x, y, z = fs // 16, (fs // 4) % 4, fs % 4
    step_a, step_b = 16 - 12 * core, 4 + 12 * core
    a, b = x + core * (y - x), y + core * (x - y)
    wide_a, wide_b = 1024 - 768 * core, 256 + 768 * core
    zz = z % 2
    pair = z // 2

    def at_a(d):
        return (rep, ((a + d) % 4) * step_a + b * step_b + z)

    def at_b(d):
        return (rep, a * step_a + ((b + d) % 4) * step_b + z)

    z_of = (z + 1 - 2 * zz, 3 - z)

    def at_z(k):
        return (rep, x * 16 + y * 4 + z_of[k])

    def at_zl(d):
        return (((zl + d) % 4) * 2 + core, fs)

    ORDER = (1, 3, 2)
    NEAR = (1, 3)
    CHUNKS = (2, 1, 3, 0)
    other_core = (zl * 2 + 1 - core, fs)

    def rdma(src, dst, send, recv, to):
        return pltpu.make_async_remote_copy(
            src_ref=src, dst_ref=dst, send_sem=send, recv_sem=recv, device_id=to, device_id_type=MESH
        )

    def rows(i, n):
        return pl.ds(pl.multiple_of(i * n, n), n)

    def channels(aa, bb, half):
        zp = half * pair + (1 - half) * (1 - pair)
        return pl.ds(pl.multiple_of(aa * wide_a + bb * wide_b + zp * 128, 128), 128)

    def lanes(bb):
        return pl.ds(pl.multiple_of(bb * 128, 128), 128)

    loads = [
        pltpu.make_async_copy(stale_ref, stl, l_in.at[0]),
        pltpu.make_async_copy(glob_ref, gin, l_in.at[1]),
        pltpu.make_async_copy(mom_ref, minn, l_in.at[2]),
        pltpu.make_async_copy(cot_ref, cotg.at[rows(a, T)], l_in.at[3]),
        pltpu.make_async_copy(w_ref, wg.at[1, pl.ds(pl.multiple_of(b * 128 + zz * 64, 64), B)], l_in.at[4]),
    ]
    for c in loads:
        c.start()
    def act_own(half, j):
        bb = (b + CHUNKS[j]) % 4
        return pltpu.make_async_copy(
            act_ref.at[:, channels(a, bb, half)], actg.at[half, rows(a, T), lanes(bb)], l_act.at[half, j]
        )

    for half in (0, 1):
        for j in range(4):
            act_own(half, j).start()

    barrier = pltpu.get_barrier_semaphore()
    greet = [at_a(d) for d in (1, 2, 3)] + [at_b(d) for d in (1, 2, 3)] + [at_z(k) for k in range(2)]
    greet += [at_zl(d) for d in (1, 2, 3)] + [other_core]
    for to in greet:
        pl.semaphore_signal(barrier, inc=1, device_id=to, device_id_type=MESH)
    pl.semaphore_wait(barrier, len(greet))

    cots = [rdma(cot_ref, cotg.at[rows(a, T)], s_cot.at[d - 1], r_cot.at[d - 1], at_a(d)) for d in (1, 2, 3)]
    for d in ORDER:
        cots[d - 1].start()

    def w_rows(zpar):
        return pl.ds(pl.multiple_of(b * 128 + zpar * 64, 64), B)

    wz = [
        rdma(w_ref, wg.at[1 if k == 0 else 0, w_rows(zz)], s_wz.at[k], r_wz.at[k], at_z(k)) for k in range(2)
    ]
    for k in range(2):
        wz[k].start()
    slots = ((1, zz), (1, 1 - zz), (0, 1 - zz), (0, zz))

    def wb(slot, k):
        half, zpar = slots[slot]
        there = wg.at[half, w_rows(zpar)]
        return rdma(w_ref if slot == 0 else there, there, s_wb.at[slot, k], r_wb.at[slot, k], at_b(NEAR[k]))

    def wb_far(slot, h):
        half, zpar = slots[slot]
        owner = (b + 3 + 2 * h) % 4
        there = wg.at[half, pl.ds(pl.multiple_of(owner * 128 + zpar * 64 + h * 32, 32), B // 2)]
        return rdma(there, there, s_wbf.at[slot, h], r_wbf.at[slot, h], at_b(NEAR[h]))

    def wb_on(slot):
        for h in (0, 1):
            wb(slot, h).wait_recv()
            wb_far(slot, h).start()

    def wb_all(slot):
        for h in (0, 1):
            wb_far(slot, h).wait_recv()

    for k in (0, 1):
        wb(0, k).start()

    def act_send(half, j, d):
        bb = (b + CHUNKS[j]) % 4
        return rdma(
            act_ref.at[:, channels((a + d) % 4, bb, half)],
            actg.at[half, rows(a, T), lanes(bb)],
            s_act.at[half, j, d - 1],
            r_act.at[half, j, d - 1],
            at_a(d),
        )

    for half in (0, 1):
        for j in range(4):
            for d in ORDER:
                act_send(half, j, d).start()

    frag = plan_ref[0] % 4
    loads[0].wait()
    picked = jnp.zeros((B, F), F32)
    for k in range(4):
        picked = jnp.where(frag == k, stl[k].astype(F32), picked)
    sel[...] = picked.astype(BF16)
    to_core = rdma(sel, selp, s_st.at[0], r_st.at[0], other_core)
    to_core.start()
    to_core.wait_recv()
    chip[...] = (sel[...].astype(F32) + selp[...].astype(F32)).reshape(4, 2, 8, F)
    scatter = [
        rdma(chip.at[(zl + d) % 4, core], rsr.at[d - 1], s_st.at[d], r_st.at[d], at_zl(d)) for d in (1, 2, 3)
    ]
    for c in scatter:
        c.start()

    def halves(h):
        return pl.ds(h * 32, B // 2)

    def chunk(half, off, zpar, h):
        to = (b + off) % 4
        return dwp.at[half, pl.ds(pl.multiple_of(to * 128 + zpar * 64 + h * 32, 32), B // 2)]

    def b_far(half, zpar, h):
        return rdma(
            chunk(half, 2, zpar, h), bfar.at[half, zpar, h], s_bf.at[half, zpar, h], r_bf.at[half, zpar, h], at_b(NEAR[h])
        )

    def b_send(half, zpar, k, h):
        return rdma(
            chunk(half, NEAR[k], zpar, h),
            brs.at[half, zpar, k, halves(h)],
            s_b.at[half, zpar, k, h],
            r_b.at[half, zpar, k, h],
            at_b(NEAR[k]),
        )

    def b_add(half, zpar):
        for h in (0, 1):
            b_far(half, zpar, h).wait_recv()
            there = chunk(half, NEAR[h], zpar, h)
            there[...] = there[...] + bfar[half, zpar, h]
            b_send(half, zpar, h, h).start()

    def weight_grad(half, first):
        for j in range(4):
            act_own(half, j).wait()
            for d in ORDER:
                act_send(half, j, d).wait_recv()
            cols = lanes((b + CHUNKS[j]) % 4)
            dwp[half, cols] = lax.dot_general(
                actg[half, :, cols], cotg[...], (((0,), (0,)), ((), ())), preferred_element_type=F32
            )
            for zpar in (first, 1 - first):
                if j == 0:
                    for h in (0, 1):
                        b_far(half, zpar, h).start()
                elif j < 3:
                    b_send(half, zpar, j - 1, 2 - j).start()

    loads[3].wait()
    for c in cots:
        c.wait_recv()
    weight_grad(0, zz)

    def part(i, zpar, h):
        return wg.at[i, pl.ds(pl.multiple_of(b * 128 + zpar * 64 + h * 32, 32), B // 2)]

    wz2 = [
        rdma(part(1 - h, 1 - zz, h), part(0, 1 - zz, h), s_wz.at[2 + h], r_wz.at[2 + h], at_z(1 - h)) for h in (0, 1)
    ]

    def pass_on(slot):
        for k in (0, 1):
            wb(slot, k).start()

    for k in (0, 1):
        wz[k].wait_recv()
        wz2[k].start()
        pass_on(k + 1)

    for c in scatter:
        c.wait_recv()
    sg[zl, core] = chip[zl, core] + rsr[0] + rsr[1] + rsr[2]
    spread = [
        rdma(sg.at[zl, core], sg.at[zl, core], s_st.at[3 + d], r_st.at[3 + d], at_zl(d)) for d in (1, 2, 3)
    ]
    for c in spread:
        c.start()

    wb_on(0)
    b_add(0, zz)
    b_add(0, 1 - zz)
    weight_grad(1, 1 - zz)
    for c in wz2:
        c.wait_recv()
    pass_on(3)
    wb_on(1)
    wb_on(2)
    b_add(1, 1 - zz)
    b_add(1, zz)

    def z_far(h):
        return rdma(zsum.at[2, halves(h)], zfar.at[h], s_zf.at[h], r_zf.at[h], at_z(1 - h))

    def z_send(k, h):
        return rdma(zsum.at[k, halves(h)], zrs.at[k, halves(h)], s_z.at[k, h], r_z.at[k, h], at_z(k))

    def over_b(half, zpar):
        for k in (0, 1):
            for h in (0, 1):
                b_send(half, zpar, k, h).wait_recv()
        mine = dwp[half, pl.ds(pl.multiple_of(b * 128 + zpar * 64, 64), B)]
        return mine + brs[half, zpar, 0] + brs[half, zpar, 1]

    def z_add(h):
        z_far(h).wait_recv()
        zsum[h, halves(h)] = zsum[h, halves(h)] + zfar[h]
        z_send(h, h).start()

    zsum[2] = over_b(0, zz)
    z_far(0).start()
    z_far(1).start()

    def ig_send(half, yy, d):
        return rdma(
            ig.at[half, rows((a + d) % 4, T), pl.ds(yy * 128, 128)],
            igrad_ref.at[:, channels(a, yy, half)],
            s_ig.at[half, d - 1],
            r_ig.at[half, d - 1],
            at_a(d),
        )

    def input_grad(half):
        ig[half] = lax.dot_general(
            cotg[...], wg[half], (((1,), (1,)), ((), ())), preferred_element_type=F32
        ).astype(BF16)
        for yy in range(4):
            for d in ORDER:
                ig_send(half, yy, d).start()
            pltpu.make_async_copy(
                ig.at[half, rows(a, T), pl.ds(yy * 128, 128)], igrad_ref.at[:, channels(a, yy, half)], l_out.at[half]
            ).start()

    loads[4].wait()
    wb_all(0)
    wb_all(1)

    wb_on(3)
    zsum[1] = over_b(0, 1 - zz)
    z_send(1, 0).start()
    zsum[0] = over_b(1, 1 - zz)
    z_send(0, 1).start()
    input_grad(1)

    wb_all(2)
    wb_all(3)
    input_grad(0)

    vp[...] = jnp.dot(actg[0], wg[0], preferred_element_type=F32) + jnp.dot(
        actg[1], wg[1], preferred_element_type=F32
    )

    def v_send(d):
        return rdma(vp.at[rows((a + d) % 4, T)], vrs.at[d - 1], s_v.at[d - 1], r_v.at[d - 1], at_a(d))

    for d in ORDER:
        v_send(d).start()

    z_add(1)
    z_add(0)

    for c in spread:
        c.wait_recv()
    across = rdma(sg.at[:, core], sg.at[:, core], s_st.at[7], r_st.at[7], other_core)
    across.start()
    across.wait_recv()
    loads[1].wait()
    loads[2].wait()
    old = jnp.zeros((B, F), F32)
    moment = jnp.zeros((B, F), F32)
    for k in range(4):
        old = jnp.where(frag == k, gin[k], old)
        moment = jnp.where(frag == k, minn[k], moment)
    mean = old - sg[...].reshape(B, F) / 8.0
    moment = 0.9 * moment + mean
    new = old - 0.7 * (mean + 0.9 * moment)
    for k in range(4):
        gout[k] = jnp.where(frag == k, new, gin[k])
        mout[k] = jnp.where(frag == k, moment, minn[k])
    stores = [
        pltpu.make_async_copy(gout, newg_ref, l_out.at[2]),
        pltpu.make_async_copy(mout, newm_ref, l_out.at[3]),
    ]
    stores[0].start()
    stores[1].start()

    zsum[3] = over_b(1, zz)

    for d in ORDER:
        v_send(d).wait_recv()
    vout[...] = (vp[rows(a, T)] + vrs[0] + vrs[1] + vrs[2]).astype(BF16)
    stores.append(pltpu.make_async_copy(vout, values_ref, l_out.at[4]))
    stores[2].start()

    for k in (0, 1):
        for h in (0, 1):
            z_send(k, h).wait_recv()
    grad = zsum[3] + zrs[0] + zrs[1]
    inner = wg[1, w_rows(zz)].astype(F32) - RATE * grad
    picked = jnp.zeros((B, F), F32)
    for k in range(4):
        picked = jnp.where(frag == k, gout[k], picked)
    wout[...] = (0.5 * inner + 0.5 * picked).astype(BF16)
    stores.append(pltpu.make_async_copy(wout, neww_ref, l_out.at[5]))
    stores[3].start()

    for half in (0, 1):
        landed = igrad_ref.at[:, pl.ds(0, 512)]
        for d in (1, 2, 3):
            own = ig.at[half, rows((a + d) % 4, T)]
            back = rdma(own, landed, s_ig.at[half, d - 1], r_ig.at[half, d - 1], at_a(d))
            back.wait_recv()
            back.wait_send()
            for j in range(4):
                act_send(half, j, d).wait_send()
        pltpu.make_async_copy(ig.at[half, rows(a, T)], landed, l_out.at[half]).wait()
    for c in cots + wz + wz2 + scatter + spread + [to_core, across]:
        c.wait_send()
    for d in (1, 2, 3):
        v_send(d).wait_send()
    for slot in range(4):
        for k in (0, 1):
            wb(slot, k).wait_send()
            wb_far(slot, k).wait_send()
    for half in (0, 1):
        for zpar in (0, 1):
            for h in (0, 1):
                b_far(half, zpar, h).wait_send()
                for k in (0, 1):
                    b_send(half, zpar, k, h).wait_send()
    for k in (0, 1):
        z_far(k).wait_send()
        for h in (0, 1):
            z_send(k, h).wait_send()
    for c in stores:
        c.wait()


def hand_out(*refs):
    ins, outs, vmem, arrived, left = refs[:5], refs[5:10], refs[10:15], refs[15], refs[16]
    come = [pltpu.make_async_copy(ins[i], vmem[i], arrived.at[i]) for i in range(5)]
    go = [pltpu.make_async_copy(vmem[i], outs[i], left.at[i]) for i in range(5)]
    for i in (1, 3, 4, 0, 2):
        come[i].start()
    for i in (1, 3, 4, 0, 2):
        come[i].wait()
        go[i].start()
    for i in range(5):
        go[i].wait()


def per_device(activations, cotangent, weights, stale_params, global_params, momentum, plan):
    anywhere = pl.BlockSpec(memory_space=pl.ANY)
    dma = pltpu.SemaphoreType.DMA
    outs = pl.pallas_call(
        kernel,
        name="diloco_step",
        out_shape=(
            jax.ShapeDtypeStruct((T, F), BF16),
            jax.ShapeDtypeStruct((T, 4096), BF16),
            jax.ShapeDtypeStruct((B, F), BF16),
            jax.ShapeDtypeStruct((4, B, F), F32),
            jax.ShapeDtypeStruct((4, B, F), F32),
        ),
        in_specs=[pl.BlockSpec(memory_space=pltpu.SMEM)] + [anywhere] * 6,
        out_specs=(anywhere,) * 5,
        scratch_shapes=[
            pltpu.VMEM((2, 512, 512), BF16),
            pltpu.VMEM((512, F), BF16),
            pltpu.VMEM((2, 512, F), BF16),
            pltpu.VMEM((2, 512, F), F32),
            pltpu.VMEM((2, 2, 2, B, F), F32),
            pltpu.VMEM((2, 2, 2, B // 2, F), F32),
            pltpu.VMEM((4, B, F), F32),
            pltpu.VMEM((2, B, F), F32),
            pltpu.VMEM((2, B // 2, F), F32),
            pltpu.VMEM((512, F), F32),
            pltpu.VMEM((3, T, F), F32),
            pltpu.VMEM((2, 512, 512), BF16),
            pltpu.VMEM((T, F), BF16),
            pltpu.VMEM((B, F), BF16),
            pltpu.VMEM((4, B, F), BF16),
            pltpu.VMEM((B, F), BF16),
            pltpu.VMEM((B, F), BF16),
            pltpu.VMEM((4, 2, 8, F), F32),
            pltpu.VMEM((3, 8, F), F32),
            pltpu.VMEM((4, 2, 8, F), F32),
            pltpu.VMEM((4, B, F), F32),
            pltpu.VMEM((4, B, F), F32),
            pltpu.VMEM((4, B, F), F32),
            pltpu.VMEM((4, B, F), F32),
            dma((3,)), dma((3,)),
            dma((2, 4, 3)), dma((2, 4, 3)),
            dma((4,)), dma((4,)),
            dma((4, 2)), dma((4, 2)),
            dma((4, 2)), dma((4, 2)),
            dma((2, 2, 2, 2)), dma((2, 2, 2, 2)),
            dma((2, 2, 2)), dma((2, 2, 2)),
            dma((2, 2)), dma((2, 2)),
            dma((2,)), dma((2,)),
            dma((2, 3)), dma((2, 3)),
            dma((3,)), dma((3,)),
            dma((8,)), dma((8,)),
            dma((5,)), dma((2, 4)), dma((6,)),
        ],
        compiler_params=pltpu.CompilerParams(
            collective_id=0, has_side_effects=True, vmem_limit_bytes=60 << 20
        ),
        cost_estimate=pl.CostEstimate(flops=1_700_000_000, bytes_accessed=7 << 20, transcendentals=0),
    )(plan, activations[0], cotangent[0], weights[0], stale_params[0], global_params, momentum)
    values, igrad, neww, newg, newm = pl.pallas_call(
        hand_out,
        name="hand_out",
        out_shape=tuple(jax.ShapeDtypeStruct(o.shape, o.dtype) for o in outs),
        in_specs=[anywhere] * 5,
        out_specs=(anywhere,) * 5,
        scratch_shapes=[pltpu.VMEM(o.shape, o.dtype) for o in outs] + [dma((5,)), dma((5,))],
        compiler_params=pltpu.CompilerParams(vmem_limit_bytes=60 << 20),
    )(*outs)
    return (values[None], igrad[None], neww[None], newg, newm)


def solution(mesh):
    placed = (
        P("replica", "fsdp", None),
        P("replica", "fsdp", None),
        P("replica", "fsdp", None),
        P("replica", None, "fsdp", None),
        P(None, "fsdp", None),
        P(None, "fsdp", None),
        P(),
    )
    return jax.shard_map(
        per_device,
        mesh=mesh,
        in_specs=placed,
        out_specs=(
            P("replica", "fsdp", None),
            P("replica", "fsdp", None),
            P("replica", "fsdp", None),
            P(None, "fsdp", None),
            P(None, "fsdp", None),
        ),
        check_vma=False,
    )
```

```python
import functools

import jax
import jax.numpy as jnp
from jax import lax
from jax.experimental import pallas as pl
from jax.experimental.pallas import tpu as pltpu
from jax.sharding import PartitionSpec as P

MESH = pl.DeviceIdType.MESH
F32 = jnp.float32
BF16 = jnp.bfloat16
T = 128
F = 512
B = 64
RATE = 0.0002


def kernel(
    plan_ref, act_ref, cot_ref, w_ref, stale_ref, glob_ref, mom_ref,
    values_ref, igrad_ref, neww_ref, newg_ref, newm_ref,
    actg, cotg, wg, dwp, brs, bfar, bdir, zsum, zrs, zfar, vp, vrs, ig, vout, wout,
    stl, sel, selp, chip, rsr, sg, gin, minn, gout, mout,
    s_cot, r_cot, s_act, r_act, s_wz, r_wz, s_wb, r_wb, s_wbf, r_wbf, s_b, r_b, s_bf, r_bf, s_bd, r_bd, s_z, r_z, s_zf, r_zf,
    s_ig, r_ig, s_v, r_v, s_st, r_st, l_in, l_act, l_out,
):
    rep = lax.axis_index("replica")
    fs = lax.axis_index("fsdp")
    zl, core = rep // 2, rep % 2
    x, y, z = fs // 16, (fs // 4) % 4, fs % 4
    step_a, step_b = 16 - 12 * core, 4 + 12 * core
    a, b = x + core * (y - x), y + core * (x - y)
    wide_a, wide_b = 1024 - 768 * core, 256 + 768 * core
    zz = z % 2
    pair = z // 2

    def at_a(d):
        return (rep, ((a + d) % 4) * step_a + b * step_b + z)

    def at_b(d):
        return (rep, a * step_a + ((b + d) % 4) * step_b + z)

    z_of = (z + 1 - 2 * zz, 3 - z)

    def at_z(k):
        return (rep, x * 16 + y * 4 + z_of[k])

    def at_zl(d):
        return (((zl + d) % 4) * 2 + core, fs)

    ORDER = (1, 3, 2)
    NEAR = (1, 3)
    CHUNKS = (2, 1, 3, 0)
    other_core = (zl * 2 + 1 - core, fs)

    def rdma(src, dst, send, recv, to):
        return pltpu.make_async_remote_copy(
            src_ref=src, dst_ref=dst, send_sem=send, recv_sem=recv, device_id=to, device_id_type=MESH
        )

    def rows(i, n):
        return pl.ds(pl.multiple_of(i * n, n), n)

    def channels(aa, bb, half):
        zp = half * pair + (1 - half) * (1 - pair)
        return pl.ds(pl.multiple_of(aa * wide_a + bb * wide_b + zp * 128, 128), 128)

    def lanes(bb):
        return pl.ds(pl.multiple_of(bb * 128, 128), 128)

    loads = [
        pltpu.make_async_copy(stale_ref, stl, l_in.at[0]),
        pltpu.make_async_copy(glob_ref, gin, l_in.at[1]),
        pltpu.make_async_copy(mom_ref, minn, l_in.at[2]),
        pltpu.make_async_copy(cot_ref, cotg.at[rows(a, T)], l_in.at[3]),
        pltpu.make_async_copy(w_ref, wg.at[1, pl.ds(pl.multiple_of(b * 128 + zz * 64, 64), B)], l_in.at[4]),
    ]
    for c in loads:
        c.start()
    def act_own(half, j):
        bb = (b + CHUNKS[j]) % 4
        return pltpu.make_async_copy(
            act_ref.at[:, channels(a, bb, half)], actg.at[half, rows(a, T), lanes(bb)], l_act.at[half, j]
        )

    for half in (0, 1):
        for j in range(4):
            act_own(half, j).start()

    barrier = pltpu.get_barrier_semaphore()
    greet = [at_a(d) for d in (1, 2, 3)] + [at_b(d) for d in (1, 2, 3)] + [at_z(k) for k in range(2)]
    greet += [at_zl(d) for d in (1, 2, 3)] + [other_core]
    for to in greet:
        pl.semaphore_signal(barrier, inc=1, device_id=to, device_id_type=MESH)
    pl.semaphore_wait(barrier, len(greet))

    cots = [rdma(cot_ref, cotg.at[rows(a, T)], s_cot.at[d - 1], r_cot.at[d - 1], at_a(d)) for d in (1, 2, 3)]
    for d in ORDER:
        cots[d - 1].start()

    def w_rows(zpar):
        return pl.ds(pl.multiple_of(b * 128 + zpar * 64, 64), B)

    wz = [
        rdma(w_ref, wg.at[1 if k == 0 else 0, w_rows(zz)], s_wz.at[k], r_wz.at[k], at_z(k)) for k in range(2)
    ]
    for k in range(2):
        wz[k].start()
    slots = ((1, zz), (1, 1 - zz), (0, 1 - zz), (0, zz))

    def wb(slot, k):
        half, zpar = slots[slot]
        there = wg.at[half, w_rows(zpar)]
        return rdma(w_ref if slot == 0 else there, there, s_wb.at[slot, k], r_wb.at[slot, k], at_b(NEAR[k]))

    def wb_far(slot, h):
        half, zpar = slots[slot]
        owner = (b + 3 + 2 * h) % 4
        there = wg.at[half, pl.ds(pl.multiple_of(owner * 128 + zpar * 64 + h * 32, 32), B // 2)]
        return rdma(there, there, s_wbf.at[slot, h], r_wbf.at[slot, h], at_b(NEAR[h]))

    def wb_on(slot):
        for h in (0, 1):
            wb(slot, h).wait_recv()
            wb_far(slot, h).start()

    def wb_all(slot):
        for h in (0, 1):
            wb_far(slot, h).wait_recv()

    for k in (0, 1):
        wb(0, k).start()

    def act_send(half, j, d):
        bb = (b + CHUNKS[j]) % 4
        return rdma(
            act_ref.at[:, channels((a + d) % 4, bb, half)],
            actg.at[half, rows(a, T), lanes(bb)],
            s_act.at[half, j, d - 1],
            r_act.at[half, j, d - 1],
            at_a(d),
        )

    for half in (0, 1):
        for j in range(4):
            for d in ORDER:
                act_send(half, j, d).start()

    frag = plan_ref[0] % 4
    loads[0].wait()
    picked = jnp.zeros((B, F), F32)
    for k in range(4):
        picked = jnp.where(frag == k, stl[k].astype(F32), picked)
    sel[...] = picked.astype(BF16)
    to_core = rdma(sel, selp, s_st.at[0], r_st.at[0], other_core)
    to_core.start()
    to_core.wait_recv()
    chip[...] = (sel[...].astype(F32) + selp[...].astype(F32)).reshape(4, 2, 8, F)
    scatter = [
        rdma(chip.at[(zl + d) % 4, core], rsr.at[d - 1], s_st.at[d], r_st.at[d], at_zl(d)) for d in (1, 2, 3)
    ]
    for c in scatter:
        c.start()

    def halves(h):
        return pl.ds(h * 32, B // 2)

    def chunk(half, off, zpar, h):
        to = (b + off) % 4
        return dwp.at[half, pl.ds(pl.multiple_of(to * 128 + zpar * 64 + h * 32, 32), B // 2)]

    def b_far(half, zpar, h):
        return rdma(
            chunk(half, 2, zpar, h), bfar.at[half, zpar, h], s_bf.at[half, zpar, h], r_bf.at[half, zpar, h], at_b(NEAR[h])
        )

    def b_send(half, zpar, k, h):
        return rdma(
            chunk(half, NEAR[k], zpar, h),
            brs.at[half, zpar, k, halves(h)],
            s_b.at[half, zpar, k, h],
            r_b.at[half, zpar, k, h],
            at_b(NEAR[k]),
        )

    def b_add(half, zpar):
        for h in (0, 1):
            b_far(half, zpar, h).wait_recv()
            there = chunk(half, NEAR[h], zpar, h)
            there[...] = there[...] + bfar[half, zpar, h]
            b_send(half, zpar, h, h).start()

    def b_direct(h, j):
        return rdma(
            chunk(1, CHUNKS[j], 1 - zz, h), bdir.at[h, j], s_bd.at[h, j], r_bd.at[h, j], at_b(CHUNKS[j])
        )

    def over_b_direct(h):
        for j in range(3):
            b_direct(h, j).wait_recv()
        return chunk(1, 0, 1 - zz, h)[...] + bdir[h, 0] + bdir[h, 1] + bdir[h, 2]

    def weight_grad(half, first):
        for j in range(4):
            act_own(half, j).wait()
            for d in ORDER:
                act_send(half, j, d).wait_recv()
            cols = lanes((b + CHUNKS[j]) % 4)
            dwp[half, cols] = lax.dot_general(
                actg[half, :, cols], cotg[...], (((0,), (0,)), ((), ())), preferred_element_type=F32
            )
            for zpar in (first, 1 - first)[half:]:
                if j == 0:
                    for h in (0, 1):
                        b_far(half, zpar, h).start()
                elif j < 3:
                    b_send(half, zpar, j - 1, 2 - j).start()
            if half == 1 and j < 3:
                for h in (1, 0):
                    b_direct(h, j).start()

    loads[3].wait()
    for c in cots:
        c.wait_recv()
    weight_grad(0, zz)

    def part(i, zpar, h):
        return wg.at[i, pl.ds(pl.multiple_of(b * 128 + zpar * 64 + h * 32, 32), B // 2)]

    wz2 = [
        rdma(part(1 - h, 1 - zz, h), part(0, 1 - zz, h), s_wz.at[2 + h], r_wz.at[2 + h], at_z(1 - h)) for h in (0, 1)
    ]

    def pass_on(slot):
        for k in (0, 1):
            wb(slot, k).start()

    for k in (0, 1):
        wz[k].wait_recv()
        wz2[k].start()
        pass_on(k + 1)

    for c in scatter:
        c.wait_recv()
    sg[zl, core] = chip[zl, core] + rsr[0] + rsr[1] + rsr[2]
    spread = [
        rdma(sg.at[zl, core], sg.at[zl, core], s_st.at[3 + d], r_st.at[3 + d], at_zl(d)) for d in (1, 2, 3)
    ]
    for c in spread:
        c.start()

    wb_on(0)
    b_add(0, zz)
    b_add(0, 1 - zz)
    weight_grad(1, 1 - zz)
    for c in wz2:
        c.wait_recv()
    pass_on(3)
    wb_on(1)
    wb_on(2)

    def z_far(h):
        return rdma(zsum.at[2, halves(h)], zfar.at[h], s_zf.at[h], r_zf.at[h], at_z(1 - h))

    def z_send(k, h):
        return rdma(zsum.at[k, halves(h)], zrs.at[k, halves(h)], s_z.at[k, h], r_z.at[k, h], at_z(k))

    def over_b(half, zpar):
        for k in (0, 1):
            for h in (0, 1):
                b_send(half, zpar, k, h).wait_recv()
        mine = dwp[half, pl.ds(pl.multiple_of(b * 128 + zpar * 64, 64), B)]
        return mine + brs[half, zpar, 0] + brs[half, zpar, 1]

    def z_add(h):
        z_far(h).wait_recv()
        zsum[h, halves(h)] = zsum[h, halves(h)] + zfar[h]
        z_send(h, h).start()

    zsum[2] = over_b(0, zz)
    z_far(0).start()
    z_far(1).start()

    def ig_send(half, yy, d):
        return rdma(
            ig.at[half, rows((a + d) % 4, T), pl.ds(yy * 128, 128)],
            igrad_ref.at[:, channels(a, yy, half)],
            s_ig.at[half, d - 1],
            r_ig.at[half, d - 1],
            at_a(d),
        )

    def input_grad(half):
        ig[half] = lax.dot_general(
            cotg[...], wg[half], (((1,), (1,)), ((), ())), preferred_element_type=F32
        ).astype(BF16)
        for yy in range(4):
            for d in ORDER:
                ig_send(half, yy, d).start()
            pltpu.make_async_copy(
                ig.at[half, rows(a, T), pl.ds(yy * 128, 128)], igrad_ref.at[:, channels(a, yy, half)], l_out.at[half]
            ).start()

    loads[4].wait()
    wb_all(0)
    wb_all(1)

    wb_on(3)
    zsum[1] = over_b(0, 1 - zz)
    z_send(1, 0).start()
    zsum[0, halves(1)] = over_b_direct(1)
    z_send(0, 1).start()
    zsum[0, halves(0)] = over_b_direct(0)
    b_add(1, zz)
    input_grad(1)

    wb_all(2)
    wb_all(3)
    input_grad(0)

    vp[...] = jnp.dot(actg[0], wg[0], preferred_element_type=F32) + jnp.dot(
        actg[1], wg[1], preferred_element_type=F32
    )

    def v_send(d):
        return rdma(vp.at[rows((a + d) % 4, T)], vrs.at[d - 1], s_v.at[d - 1], r_v.at[d - 1], at_a(d))

    for d in ORDER:
        v_send(d).start()

    z_add(1)
    z_add(0)

    for c in spread:
        c.wait_recv()
    across = rdma(sg.at[:, core], sg.at[:, core], s_st.at[7], r_st.at[7], other_core)
    across.start()
    across.wait_recv()
    loads[1].wait()
    loads[2].wait()
    old = jnp.zeros((B, F), F32)
    moment = jnp.zeros((B, F), F32)
    for k in range(4):
        old = jnp.where(frag == k, gin[k], old)
        moment = jnp.where(frag == k, minn[k], moment)
    mean = old - sg[...].reshape(B, F) / 8.0
    moment = 0.9 * moment + mean
    new = old - 0.7 * (mean + 0.9 * moment)
    for k in range(4):
        gout[k] = jnp.where(frag == k, new, gin[k])
        mout[k] = jnp.where(frag == k, moment, minn[k])
    stores = [
        pltpu.make_async_copy(gout, newg_ref, l_out.at[2]),
        pltpu.make_async_copy(mout, newm_ref, l_out.at[3]),
    ]
    stores[0].start()
    stores[1].start()

    zsum[3] = over_b(1, zz)

    for d in ORDER:
        v_send(d).wait_recv()
    vout[...] = (vp[rows(a, T)] + vrs[0] + vrs[1] + vrs[2]).astype(BF16)
    stores.append(pltpu.make_async_copy(vout, values_ref, l_out.at[4]))
    stores[2].start()

    for k in (0, 1):
        for h in (0, 1):
            z_send(k, h).wait_recv()
    grad = zsum[3] + zrs[0] + zrs[1]
    inner = wg[1, w_rows(zz)].astype(F32) - RATE * grad
    picked = jnp.zeros((B, F), F32)
    for k in range(4):
        picked = jnp.where(frag == k, gout[k], picked)
    wout[...] = (0.5 * inner + 0.5 * picked).astype(BF16)
    stores.append(pltpu.make_async_copy(wout, neww_ref, l_out.at[5]))
    stores[3].start()

    for half in (0, 1):
        landed = igrad_ref.at[:, pl.ds(0, 512)]
        for d in (1, 2, 3):
            own = ig.at[half, rows((a + d) % 4, T)]
            back = rdma(own, landed, s_ig.at[half, d - 1], r_ig.at[half, d - 1], at_a(d))
            back.wait_recv()
            back.wait_send()
            for j in range(4):
                act_send(half, j, d).wait_send()
        pltpu.make_async_copy(ig.at[half, rows(a, T)], landed, l_out.at[half]).wait()
    for c in cots + wz + wz2 + scatter + spread + [to_core, across]:
        c.wait_send()
    for d in (1, 2, 3):
        v_send(d).wait_send()
    for slot in range(4):
        for k in (0, 1):
            wb(slot, k).wait_send()
            wb_far(slot, k).wait_send()
    for half, zpar in ((0, zz), (0, 1 - zz), (1, zz)):
        for h in (0, 1):
            b_far(half, zpar, h).wait_send()
            for k in (0, 1):
                b_send(half, zpar, k, h).wait_send()
    for h in (0, 1):
        for j in range(3):
            b_direct(h, j).wait_send()
    for k in (0, 1):
        z_far(k).wait_send()
        for h in (0, 1):
            z_send(k, h).wait_send()
    for c in stores:
        c.wait()


def hand_out(*refs):
    ins, outs, vmem, arrived, left = refs[:5], refs[5:10], refs[10:15], refs[15], refs[16]
    parts = [(1, pl.ds(k * 32, 32)) for k in range(4)] + [(3, slice(None)), (4, slice(None)), (0, slice(None)), (2, slice(None))]
    come = [pltpu.make_async_copy(ins[i].at[p], vmem[i].at[p], arrived.at[n]) for n, (i, p) in enumerate(parts)]
    go = [pltpu.make_async_copy(vmem[i].at[p], outs[i].at[p], left.at[n]) for n, (i, p) in enumerate(parts)]
    for c in come:
        c.start()
    for c, d in zip(come, go):
        c.wait()
        d.start()
    for d in go:
        d.wait()


def per_device(activations, cotangent, weights, stale_params, global_params, momentum, plan):
    anywhere = pl.BlockSpec(memory_space=pl.ANY)
    dma = pltpu.SemaphoreType.DMA
    outs = pl.pallas_call(
        kernel,
        name="diloco_step",
        out_shape=(
            jax.ShapeDtypeStruct((T, F), BF16),
            jax.ShapeDtypeStruct((T, 4096), BF16),
            jax.ShapeDtypeStruct((B, F), BF16),
            jax.ShapeDtypeStruct((4, B, F), F32),
            jax.ShapeDtypeStruct((4, B, F), F32),
        ),
        in_specs=[pl.BlockSpec(memory_space=pltpu.SMEM)] + [anywhere] * 6,
        out_specs=(anywhere,) * 5,
        scratch_shapes=[
            pltpu.VMEM((2, 512, 512), BF16),
            pltpu.VMEM((512, F), BF16),
            pltpu.VMEM((2, 512, F), BF16),
            pltpu.VMEM((2, 512, F), F32),
            pltpu.VMEM((2, 2, 2, B, F), F32),
            pltpu.VMEM((2, 2, 2, B // 2, F), F32),
            pltpu.VMEM((2, 3, B // 2, F), F32),
            pltpu.VMEM((4, B, F), F32),
            pltpu.VMEM((2, B, F), F32),
            pltpu.VMEM((2, B // 2, F), F32),
            pltpu.VMEM((512, F), F32),
            pltpu.VMEM((3, T, F), F32),
            pltpu.VMEM((2, 512, 512), BF16),
            pltpu.VMEM((T, F), BF16),
            pltpu.VMEM((B, F), BF16),
            pltpu.VMEM((4, B, F), BF16),
            pltpu.VMEM((B, F), BF16),
            pltpu.VMEM((B, F), BF16),
            pltpu.VMEM((4, 2, 8, F), F32),
            pltpu.VMEM((3, 8, F), F32),
            pltpu.VMEM((4, 2, 8, F), F32),
            pltpu.VMEM((4, B, F), F32),
            pltpu.VMEM((4, B, F), F32),
            pltpu.VMEM((4, B, F), F32),
            pltpu.VMEM((4, B, F), F32),
            dma((3,)), dma((3,)),
            dma((2, 4, 3)), dma((2, 4, 3)),
            dma((4,)), dma((4,)),
            dma((4, 2)), dma((4, 2)),
            dma((4, 2)), dma((4, 2)),
            dma((2, 2, 2, 2)), dma((2, 2, 2, 2)),
            dma((2, 2, 2)), dma((2, 2, 2)),
            dma((2, 3)), dma((2, 3)),
            dma((2, 2)), dma((2, 2)),
            dma((2,)), dma((2,)),
            dma((2, 3)), dma((2, 3)),
            dma((3,)), dma((3,)),
            dma((8,)), dma((8,)),
            dma((5,)), dma((2, 4)), dma((6,)),
        ],
        compiler_params=pltpu.CompilerParams(
            collective_id=0, has_side_effects=True, vmem_limit_bytes=60 << 20
        ),
        cost_estimate=pl.CostEstimate(flops=1_700_000_000, bytes_accessed=7 << 20, transcendentals=0),
    )(plan, activations[0], cotangent[0], weights[0], stale_params[0], global_params, momentum)
    values, igrad, neww, newg, newm = pl.pallas_call(
        hand_out,
        name="hand_out",
        out_shape=tuple(jax.ShapeDtypeStruct(o.shape, o.dtype) for o in outs),
        in_specs=[anywhere] * 5,
        out_specs=(anywhere,) * 5,
        scratch_shapes=[pltpu.VMEM(o.shape, o.dtype) for o in outs] + [dma((8,)), dma((8,))],
        compiler_params=pltpu.CompilerParams(vmem_limit_bytes=60 << 20),
    )(*outs)
    return (values[None], igrad[None], neww[None], newg, newm)


def solution(mesh):
    placed = (
        P("replica", "fsdp", None),
        P("replica", "fsdp", None),
        P("replica", "fsdp", None),
        P("replica", None, "fsdp", None),
        P(None, "fsdp", None),
        P(None, "fsdp", None),
        P(),
    )
    return jax.shard_map(
        per_device,
        mesh=mesh,
        in_specs=placed,
        out_specs=(
            P("replica", "fsdp", None),
            P("replica", "fsdp", None),
            P("replica", "fsdp", None),
            P(None, "fsdp", None),
            P(None, "fsdp", None),
        ),
        check_vma=False,
    )
```

```python
import functools

import jax
import jax.numpy as jnp
from jax import lax
from jax.experimental import pallas as pl
from jax.experimental.pallas import tpu as pltpu
from jax.sharding import PartitionSpec as P

MESH = pl.DeviceIdType.MESH
F32 = jnp.float32
BF16 = jnp.bfloat16
T = 128
F = 512
B = 64
RATE = 0.0002


def kernel(
    plan_ref, act_ref, cot_ref, w_ref, stale_ref, glob_ref, mom_ref,
    values_ref, igrad_ref, neww_ref, newg_ref, newm_ref,
    actg, cotg, wg, dwp, brs, bfar, bdir, zsum, zrs, zfar, vp, vrs, ig, vout, wout,
    stl, sel, selp, chip, rsr, sg, gin, minn, gout, mout,
    s_cot, r_cot, s_act, r_act, s_wz, r_wz, s_wb, r_wb, s_wbf, r_wbf, s_b, r_b, s_bf, r_bf, s_bd, r_bd, s_z, r_z, s_zf, r_zf,
    s_ig, r_ig, s_v, r_v, s_st, r_st, l_in, l_act, l_out,
):
    rep = lax.axis_index("replica")
    fs = lax.axis_index("fsdp")
    zl, core = rep // 2, rep % 2
    x, y, z = fs // 16, (fs // 4) % 4, fs % 4
    step_a, step_b = 16 - 12 * core, 4 + 12 * core
    a, b = x + core * (y - x), y + core * (x - y)
    wide_a, wide_b = 1024 - 768 * core, 256 + 768 * core
    zz = z % 2
    pair = z // 2

    def at_a(d):
        return (rep, ((a + d) % 4) * step_a + b * step_b + z)

    def at_b(d):
        return (rep, a * step_a + ((b + d) % 4) * step_b + z)

    z_of = (z + 1 - 2 * zz, 3 - z)

    def at_z(k):
        return (rep, x * 16 + y * 4 + z_of[k])

    def at_zl(d):
        return (((zl + d) % 4) * 2 + core, fs)

    ORDER = (1, 3, 2)
    NEAR = (1, 3)
    CHUNKS = (2, 1, 3, 0)
    other_core = (zl * 2 + 1 - core, fs)

    def rdma(src, dst, send, recv, to):
        return pltpu.make_async_remote_copy(
            src_ref=src, dst_ref=dst, send_sem=send, recv_sem=recv, device_id=to, device_id_type=MESH
        )

    def rows(i, n):
        return pl.ds(pl.multiple_of(i * n, n), n)

    def channels(aa, bb, half):
        zp = half * pair + (1 - half) * (1 - pair)
        return pl.ds(pl.multiple_of(aa * wide_a + bb * wide_b + zp * 128, 128), 128)

    def lanes(bb):
        return pl.ds(pl.multiple_of(bb * 128, 128), 128)

    loads = [
        pltpu.make_async_copy(stale_ref, stl, l_in.at[0]),
        pltpu.make_async_copy(glob_ref, gin, l_in.at[1]),
        pltpu.make_async_copy(mom_ref, minn, l_in.at[2]),
        pltpu.make_async_copy(cot_ref, cotg.at[rows(a, T)], l_in.at[3]),
        pltpu.make_async_copy(w_ref, wg.at[1, pl.ds(pl.multiple_of(b * 128 + zz * 64, 64), B)], l_in.at[4]),
    ]
    for c in loads:
        c.start()
    def act_own(half, j):
        bb = (b + CHUNKS[j]) % 4
        return pltpu.make_async_copy(
            act_ref.at[:, channels(a, bb, half)], actg.at[half, rows(a, T), lanes(bb)], l_act.at[half, j]
        )

    for half in (0, 1):
        for j in range(4):
            act_own(half, j).start()

    barrier = pltpu.get_barrier_semaphore()
    greet = [at_a(d) for d in (1, 2, 3)] + [at_b(d) for d in (1, 2, 3)] + [at_z(k) for k in range(2)]
    greet += [at_zl(d) for d in (1, 2, 3)] + [other_core]
    for to in greet:
        pl.semaphore_signal(barrier, inc=1, device_id=to, device_id_type=MESH)
    pl.semaphore_wait(barrier, len(greet))

    cots = [rdma(cot_ref, cotg.at[rows(a, T)], s_cot.at[d - 1], r_cot.at[d - 1], at_a(d)) for d in (1, 2, 3)]
    for d in ORDER:
        cots[d - 1].start()

    def w_rows(zpar):
        return pl.ds(pl.multiple_of(b * 128 + zpar * 64, 64), B)

    wz = [
        rdma(w_ref, wg.at[1 if k == 0 else 0, w_rows(zz)], s_wz.at[k], r_wz.at[k], at_z(k)) for k in range(2)
    ]
    for k in range(2):
        wz[k].start()
    slots = ((1, zz), (1, 1 - zz), (0, 1 - zz), (0, zz))

    def wb(slot, k):
        half, zpar = slots[slot]
        there = wg.at[half, w_rows(zpar)]
        return rdma(w_ref if slot == 0 else there, there, s_wb.at[slot, k], r_wb.at[slot, k], at_b(NEAR[k]))

    def wb_far(slot, h):
        half, zpar = slots[slot]
        owner = (b + 3 + 2 * h) % 4
        there = wg.at[half, pl.ds(pl.multiple_of(owner * 128 + zpar * 64 + h * 32, 32), B // 2)]
        return rdma(there, there, s_wbf.at[slot, h], r_wbf.at[slot, h], at_b(NEAR[h]))

    def wb_on(slot):
        for h in (0, 1):
            wb(slot, h).wait_recv()
            wb_far(slot, h).start()

    def wb_all(slot):
        for h in (0, 1):
            wb_far(slot, h).wait_recv()

    for k in (0, 1):
        wb(0, k).start()

    def act_send(half, j, d):
        bb = (b + CHUNKS[j]) % 4
        return rdma(
            act_ref.at[:, channels((a + d) % 4, bb, half)],
            actg.at[half, rows(a, T), lanes(bb)],
            s_act.at[half, j, d - 1],
            r_act.at[half, j, d - 1],
            at_a(d),
        )

    for half in (0, 1):
        for j in range(4):
            for d in ORDER:
                act_send(half, j, d).start()

    frag = plan_ref[0] % 4
    loads[0].wait()
    picked = jnp.zeros((B, F), F32)
    for k in range(4):
        picked = jnp.where(frag == k, stl[k].astype(F32), picked)
    sel[...] = picked.astype(BF16)
    to_core = rdma(sel, selp, s_st.at[0], r_st.at[0], other_core)
    to_core.start()
    to_core.wait_recv()
    chip[...] = (sel[...].astype(F32) + selp[...].astype(F32)).reshape(4, 2, 8, F)
    scatter = [
        rdma(chip.at[(zl + d) % 4, core], rsr.at[d - 1], s_st.at[d], r_st.at[d], at_zl(d)) for d in (1, 2, 3)
    ]
    for c in scatter:
        c.start()

    def halves(h):
        return pl.ds(h * 32, B // 2)

    def chunk(half, off, zpar, h):
        to = (b + off) % 4
        return dwp.at[half, pl.ds(pl.multiple_of(to * 128 + zpar * 64 + h * 32, 32), B // 2)]

    def b_far(half, zpar, h):
        return rdma(
            chunk(half, 2, zpar, h), bfar.at[half, zpar, h], s_bf.at[half, zpar, h], r_bf.at[half, zpar, h], at_b(NEAR[h])
        )

    def b_send(half, zpar, k, h):
        return rdma(
            chunk(half, NEAR[k], zpar, h),
            brs.at[half, zpar, k, halves(h)],
            s_b.at[half, zpar, k, h],
            r_b.at[half, zpar, k, h],
            at_b(NEAR[k]),
        )

    def b_add(half, zpar):
        for h in (0, 1):
            b_far(half, zpar, h).wait_recv()
            there = chunk(half, NEAR[h], zpar, h)
            there[...] = there[...] + bfar[half, zpar, h]
            b_send(half, zpar, h, h).start()

    def b_direct(h, j):
        return rdma(
            chunk(1, CHUNKS[j], 1 - zz, h), bdir.at[h, j], s_bd.at[h, j], r_bd.at[h, j], at_b(CHUNKS[j])
        )

    def over_b_direct(h):
        for j in range(3):
            b_direct(h, j).wait_recv()
        return chunk(1, 0, 1 - zz, h)[...] + bdir[h, 0] + bdir[h, 1] + bdir[h, 2]

    def weight_grad(half, first):
        for j in range(4):
            act_own(half, j).wait()
            for d in ORDER:
                act_send(half, j, d).wait_recv()
            cols = lanes((b + CHUNKS[j]) % 4)
            dwp[half, cols] = lax.dot_general(
                actg[half, :, cols], cotg[...], (((0,), (0,)), ((), ())), preferred_element_type=F32
            )
            for zpar in (first, 1 - first)[half:]:
                if j == 0:
                    for h in (0, 1):
                        b_far(half, zpar, h).start()
                elif j < 3:
                    b_send(half, zpar, j - 1, 2 - j).start()
            if half == 1 and j < 3:
                for h in (1, 0):
                    b_direct(h, j).start()

    loads[3].wait()
    for c in cots:
        c.wait_recv()
    weight_grad(0, zz)

    def part(i, zpar, h):
        return wg.at[i, pl.ds(pl.multiple_of(b * 128 + zpar * 64 + h * 32, 32), B // 2)]

    wz2 = [
        rdma(part(1 - h, 1 - zz, h), part(0, 1 - zz, h), s_wz.at[2 + h], r_wz.at[2 + h], at_z(1 - h)) for h in (0, 1)
    ]

    def pass_on(slot):
        for k in (0, 1):
            wb(slot, k).start()

    for k in (0, 1):
        wz[k].wait_recv()
        wz2[k].start()
        pass_on(k + 1)

    for c in scatter:
        c.wait_recv()
    sg[zl, core] = chip[zl, core] + rsr[0] + rsr[1] + rsr[2]
    spread = [
        rdma(sg.at[zl, core], sg.at[zl, core], s_st.at[3 + d], r_st.at[3 + d], at_zl(d)) for d in (1, 2, 3)
    ]
    for c in spread:
        c.start()

    wb_on(0)
    b_add(0, zz)
    b_add(0, 1 - zz)
    weight_grad(1, 1 - zz)
    for c in wz2:
        c.wait_recv()
    pass_on(3)
    wb_on(1)
    wb_on(2)

    def z_far(h):
        return rdma(zsum.at[2, halves(h)], zfar.at[h], s_zf.at[h], r_zf.at[h], at_z(1 - h))

    def z_send(k, h):
        return rdma(zsum.at[k, halves(h)], zrs.at[k, halves(h)], s_z.at[k, h], r_z.at[k, h], at_z(k))

    def over_b(half, zpar):
        for k in (0, 1):
            for h in (0, 1):
                b_send(half, zpar, k, h).wait_recv()
        mine = dwp[half, pl.ds(pl.multiple_of(b * 128 + zpar * 64, 64), B)]
        return mine + brs[half, zpar, 0] + brs[half, zpar, 1]

    def z_add(h):
        z_far(h).wait_recv()
        zsum[h, halves(h)] = zsum[h, halves(h)] + zfar[h]
        z_send(h, h).start()

    zsum[2] = over_b(0, zz)
    z_far(0).start()
    z_far(1).start()

    def ig_send(half, yy, d):
        return rdma(
            ig.at[half, rows((a + d) % 4, T), pl.ds(yy * 128, 128)],
            igrad_ref.at[:, channels(a, yy, half)],
            s_ig.at[half, d - 1],
            r_ig.at[half, d - 1],
            at_a(d),
        )

    def input_grad(half):
        ig[half] = lax.dot_general(
            cotg[...], wg[half], (((1,), (1,)), ((), ())), preferred_element_type=F32
        ).astype(BF16)
        for yy in range(4):
            for d in ORDER:
                ig_send(half, yy, d).start()
            pltpu.make_async_copy(
                ig.at[half, rows(a, T), pl.ds(yy * 128, 128)], igrad_ref.at[:, channels(a, yy, half)], l_out.at[half]
            ).start()

    loads[4].wait()
    wb_all(0)
    wb_all(1)

    wb_on(3)
    zsum[1] = over_b(0, 1 - zz)
    z_send(1, 0).start()
    zsum[0, halves(1)] = over_b_direct(1)
    z_send(0, 1).start()
    zsum[0, halves(0)] = over_b_direct(0)
    b_add(1, zz)
    input_grad(1)

    wb_all(2)
    wb_all(3)
    input_grad(0)

    vp[...] = jnp.dot(actg[0], wg[0], preferred_element_type=F32) + jnp.dot(
        actg[1], wg[1], preferred_element_type=F32
    )

    def v_send(d):
        return rdma(vp.at[rows((a + d) % 4, T)], vrs.at[d - 1], s_v.at[d - 1], r_v.at[d - 1], at_a(d))

    for d in ORDER:
        v_send(d).start()

    z_add(1)
    z_add(0)

    for c in spread:
        c.wait_recv()
    across = rdma(sg.at[:, core], sg.at[:, core], s_st.at[7], r_st.at[7], other_core)
    across.start()
    across.wait_recv()
    loads[1].wait()
    loads[2].wait()
    old = jnp.zeros((B, F), F32)
    moment = jnp.zeros((B, F), F32)
    for k in range(4):
        old = jnp.where(frag == k, gin[k], old)
        moment = jnp.where(frag == k, minn[k], moment)
    mean = old - sg[...].reshape(B, F) / 8.0
    moment = 0.9 * moment + mean
    new = old - 0.7 * (mean + 0.9 * moment)
    for k in range(4):
        gout[k] = jnp.where(frag == k, new, gin[k])
        mout[k] = jnp.where(frag == k, moment, minn[k])
    stores = [
        pltpu.make_async_copy(gout, newg_ref, l_out.at[2]),
        pltpu.make_async_copy(mout, newm_ref, l_out.at[3]),
    ]
    stores[0].start()
    stores[1].start()

    zsum[3] = over_b(1, zz)

    for c in cots + wz + wz2 + scatter + spread + [to_core, across]:
        c.wait_send()
    for slot in range(4):
        for k in (0, 1):
            wb(slot, k).wait_send()
            wb_far(slot, k).wait_send()
    for half, zpar in ((0, zz), (0, 1 - zz), (1, zz)):
        for h in (0, 1):
            b_far(half, zpar, h).wait_send()
            for k in (0, 1):
                b_send(half, zpar, k, h).wait_send()
    for h in (0, 1):
        for j in range(3):
            b_direct(h, j).wait_send()
    for half in (0, 1):
        for d in (1, 2, 3):
            for j in range(4):
                act_send(half, j, d).wait_send()

    for d in ORDER:
        v_send(d).wait_recv()
    vout[...] = (vp[rows(a, T)] + vrs[0] + vrs[1] + vrs[2]).astype(BF16)
    stores.append(pltpu.make_async_copy(vout, values_ref, l_out.at[4]))
    stores[2].start()

    for k in (0, 1):
        for h in (0, 1):
            z_send(k, h).wait_recv()
    grad = zsum[3] + zrs[0] + zrs[1]
    inner = wg[1, w_rows(zz)].astype(F32) - RATE * grad
    picked = jnp.zeros((B, F), F32)
    for k in range(4):
        picked = jnp.where(frag == k, gout[k], picked)
    wout[...] = (0.5 * inner + 0.5 * picked).astype(BF16)
    stores.append(pltpu.make_async_copy(wout, neww_ref, l_out.at[5]))
    stores[3].start()

    for half in (0, 1):
        landed = igrad_ref.at[:, pl.ds(0, 512)]
        for d in (1, 2, 3):
            own = ig.at[half, rows((a + d) % 4, T)]
            back = rdma(own, landed, s_ig.at[half, d - 1], r_ig.at[half, d - 1], at_a(d))
            back.wait_recv()
            back.wait_send()
        pltpu.make_async_copy(ig.at[half, rows(a, T)], landed, l_out.at[half]).wait()
    for d in (1, 2, 3):
        v_send(d).wait_send()
    for k in (0, 1):
        z_far(k).wait_send()
        for h in (0, 1):
            z_send(k, h).wait_send()
    for c in stores:
        c.wait()


def hand_out(*refs):
    ins, outs, vmem, arrived, left = refs[:5], refs[5:10], refs[10:15], refs[15], refs[16]
    parts = [(1, pl.ds(k * 32, 32)) for k in range(4)] + [(3, slice(None)), (4, slice(None)), (0, slice(None)), (2, slice(None))]
    come = [pltpu.make_async_copy(ins[i].at[p], vmem[i].at[p], arrived.at[n]) for n, (i, p) in enumerate(parts)]
    go = [pltpu.make_async_copy(vmem[i].at[p], outs[i].at[p], left.at[n]) for n, (i, p) in enumerate(parts)]
    for c in come:
        c.start()
    for c, d in zip(come, go):
        c.wait()
        d.start()
    for d in go:
        d.wait()


def per_device(activations, cotangent, weights, stale_params, global_params, momentum, plan):
    anywhere = pl.BlockSpec(memory_space=pl.ANY)
    dma = pltpu.SemaphoreType.DMA
    outs = pl.pallas_call(
        kernel,
        name="diloco_step",
        out_shape=(
            jax.ShapeDtypeStruct((T, F), BF16),
            jax.ShapeDtypeStruct((T, 4096), BF16),
            jax.ShapeDtypeStruct((B, F), BF16),
            jax.ShapeDtypeStruct((4, B, F), F32),
            jax.ShapeDtypeStruct((4, B, F), F32),
        ),
        in_specs=[pl.BlockSpec(memory_space=pltpu.SMEM)] + [anywhere] * 6,
        out_specs=(anywhere,) * 5,
        scratch_shapes=[
            pltpu.VMEM((2, 512, 512), BF16),
            pltpu.VMEM((512, F), BF16),
            pltpu.VMEM((2, 512, F), BF16),
            pltpu.VMEM((2, 512, F), F32),
            pltpu.VMEM((2, 2, 2, B, F), F32),
            pltpu.VMEM((2, 2, 2, B // 2, F), F32),
            pltpu.VMEM((2, 3, B // 2, F), F32),
            pltpu.VMEM((4, B, F), F32),
            pltpu.VMEM((2, B, F), F32),
            pltpu.VMEM((2, B // 2, F), F32),
            pltpu.VMEM((512, F), F32),
            pltpu.VMEM((3, T, F), F32),
            pltpu.VMEM((2, 512, 512), BF16),
            pltpu.VMEM((T, F), BF16),
            pltpu.VMEM((B, F), BF16),
            pltpu.VMEM((4, B, F), BF16),
            pltpu.VMEM((B, F), BF16),
            pltpu.VMEM((B, F), BF16),
            pltpu.VMEM((4, 2, 8, F), F32),
            pltpu.VMEM((3, 8, F), F32),
            pltpu.VMEM((4, 2, 8, F), F32),
            pltpu.VMEM((4, B, F), F32),
            pltpu.VMEM((4, B, F), F32),
            pltpu.VMEM((4, B, F), F32),
            pltpu.VMEM((4, B, F), F32),
            dma((3,)), dma((3,)),
            dma((2, 4, 3)), dma((2, 4, 3)),
            dma((4,)), dma((4,)),
            dma((4, 2)), dma((4, 2)),
            dma((4, 2)), dma((4, 2)),
            dma((2, 2, 2, 2)), dma((2, 2, 2, 2)),
            dma((2, 2, 2)), dma((2, 2, 2)),
            dma((2, 3)), dma((2, 3)),
            dma((2, 2)), dma((2, 2)),
            dma((2,)), dma((2,)),
            dma((2, 3)), dma((2, 3)),
            dma((3,)), dma((3,)),
            dma((8,)), dma((8,)),
            dma((5,)), dma((2, 4)), dma((6,)),
        ],
        compiler_params=pltpu.CompilerParams(
            collective_id=0, has_side_effects=True, vmem_limit_bytes=60 << 20
        ),
        cost_estimate=pl.CostEstimate(flops=1_700_000_000, bytes_accessed=7 << 20, transcendentals=0),
    )(plan, activations[0], cotangent[0], weights[0], stale_params[0], global_params, momentum)
    values, igrad, neww, newg, newm = pl.pallas_call(
        hand_out,
        name="hand_out",
        out_shape=tuple(jax.ShapeDtypeStruct(o.shape, o.dtype) for o in outs),
        in_specs=[anywhere] * 5,
        out_specs=(anywhere,) * 5,
        scratch_shapes=[pltpu.VMEM(o.shape, o.dtype) for o in outs] + [dma((8,)), dma((8,))],
        compiler_params=pltpu.CompilerParams(vmem_limit_bytes=60 << 20),
    )(*outs)
    return (values[None], igrad[None], neww[None], newg, newm)


def solution(mesh):
    placed = (
        P("replica", "fsdp", None),
        P("replica", "fsdp", None),
        P("replica", "fsdp", None),
        P("replica", None, "fsdp", None),
        P(None, "fsdp", None),
        P(None, "fsdp", None),
        P(),
    )
    return jax.shard_map(
        per_device,
        mesh=mesh,
        in_specs=placed,
        out_specs=(
            P("replica", "fsdp", None),
            P("replica", "fsdp", None),
            P("replica", "fsdp", None),
            P(None, "fsdp", None),
            P(None, "fsdp", None),
        ),
        check_vma=False,
    )
```
